256 devices in a mesh: row: 32 (over x, y, z_hi), col: 8 (over z_lo, core).
Axes of the slice: x: 4, y: 4, z: 8 (z_hi: 2, z_lo: 4; z = z_hi * 4 + z_lo), core: 2. Of those that a mesh axis runs over, the one named last changes fastest.
Arguments:
- pairs: bfloat16 [64, 1024, 1024], P(None, 'row', 'col'), may hold values from -6 to 6
- weights_first: bfloat16 [3, 3, 64, 64], replicated, may hold values from -0.25 to 0.25
- weights_second: bfloat16 [3, 3, 64, 64], replicated, may hold values from -0.25 to 0.25
- gains: float32 [2, 64], replicated, may hold values from 0.5 to 1.5
- shifts: float32 [2, 64], replicated, may hold values from -3 to 3
- dilations: int32 [2], replicated, may hold values from 1 to 16, as said below
- residue_count: int32 [1], replicated, may hold values from 768 to 1024
- cotangent: bfloat16 [64, 1024, 1024], P(None, 'row', 'col'), may hold values from -6 to 6
Outputs:
- symmetric: bfloat16 [64, 1024, 1024], P(None, 'row', 'col')
- grad_pairs: bfloat16 [64, 1024, 1024], P(None, 'row', 'col')
- grad_weights: float32 [2, 3, 3, 64, 64], replicated
The draws below stay inside these ranges and needn't reach their ends.
Inputs may be any that keep to these rules, and one draw needn't show every extreme that they name: `dilations`: each is a power of two; one of the two equals 16, the other is smaller.
All inputs are finite; a program needn't handle non-finite values.
Results may differ from the reference program's by a relative error of at most 0.0054.
Values may be sent and summed in bfloat16 or wider, within the bound.
A program may use at most 128 MiB of HBM per device.

```python
import jax
import jax.numpy as jnp
from jax import lax

CHANNELS = 64
MAX_DILATION = 16
RESIDUES = 1024


def draw_dilations(key, part):
    key = jax.random.fold_in(key, 7)
    pick_key, order_key = jax.random.split(key)
    powers = jnp.array([1, 2, 4, 8], jnp.int32)
    other = powers[jax.random.randint(pick_key, (), 0, 4)]
    largest = jnp.int32(MAX_DILATION)
    flipped = jax.random.randint(order_key, (), 0, 2)
    return jnp.where(flipped == 0, jnp.stack([largest, other]), jnp.stack([other, largest])).astype(jnp.int32)


def draw_pairs(key, part):
    key = jax.random.fold_in(key, 11)
    offset_key, common_key, own_key = jax.random.split(key, 3)
    offset = jax.random.uniform(offset_key, (CHANNELS, 1, 1), jnp.float32, -1.0, 1.0)
    common = jax.random.normal(common_key, (1, RESIDUES, RESIDUES), jnp.float32)
    own = jax.random.normal(own_key, (CHANNELS, RESIDUES, RESIDUES), jnp.float32)
    field = offset + 0.6 * common + 0.8 * own
    return jnp.clip(field, -6.0, 6.0).astype(jnp.bfloat16)


def draw_cotangent(key, part):
    key = jax.random.fold_in(key, 13)
    offset_key, noise_key = jax.random.split(key)
    offset = jax.random.uniform(offset_key, (CHANNELS, 1, 1), jnp.float32, -1.5, 1.5)
    noise = jax.random.normal(noise_key, (CHANNELS, RESIDUES, RESIDUES), jnp.float32)
    field = offset + noise
    return jnp.clip(field, -6.0, 6.0).astype(jnp.bfloat16)


def scatter_about(stream_key, shape, deviation, bound, held_as=jnp.bfloat16):
    entries = deviation * jax.random.normal(stream_key, shape, jnp.float32)
    return jnp.clip(entries, min=-bound, max=bound).astype(held_as)


def setup_inputs(seed: int = 0) -> dict:
    keys = jax.random.split(jax.random.key(seed), 9)
    pairs = draw_pairs(jax.random.fold_in(keys[8], 71), 0)
    weights_first = scatter_about(keys[1], (3, 3, CHANNELS, CHANNELS), (9 * CHANNELS) ** -0.5, 0.25)
    weights_second = scatter_about(keys[2], (3, 3, CHANNELS, CHANNELS), (9 * CHANNELS) ** -0.5, 0.25)
    gains = jnp.clip(1.0 + 0.1 * jax.random.normal(keys[3], (2, CHANNELS), jnp.float32), 0.5, 1.5)
    shifts = scatter_about(keys[4], (2, CHANNELS), 0.5, 3.0, jnp.float32)
    dilations = draw_dilations(jax.random.fold_in(keys[8], 71), 0)
    residue_count = jax.random.randint(keys[6], (1,), RESIDUES - RESIDUES // 4, RESIDUES + 1).astype(jnp.int32)
    cotangent = draw_cotangent(jax.random.fold_in(keys[8], 71), 0)
    return {"pairs": pairs, "weights_first": weights_first, "weights_second": weights_second, "gains": gains, "shifts": shifts, "dilations": dilations, "residue_count": residue_count, "cotangent": cotangent}


EPSILON = 1e-05

def pad_map(field):
    return jnp.pad(field, ((0, 0), (MAX_DILATION, MAX_DILATION), (MAX_DILATION, MAX_DILATION)))

def window(padded, down, right, rows, cols):
    start_row = (MAX_DILATION + down).astype(jnp.int32)
    start_col = (MAX_DILATION + right).astype(jnp.int32)
    return lax.dynamic_slice(padded, (jnp.int32(0), start_row, start_col), (padded.shape[0], rows, cols))

def convolve(field, weights, dilation):
    chans, rows, cols = field.shape
    padded = pad_map(field)
    summed = jnp.zeros((weights.shape[2], rows * cols), jnp.float32)
    for vertical in range(3):
        for lateral in range(3):
            portion = window(padded, (vertical - 1) * dilation, (lateral - 1) * dilation, rows, cols)
            summed = summed + jnp.dot(weights[vertical, lateral], portion.reshape(chans, rows * cols), preferred_element_type=jnp.float32)
    return summed.reshape(weights.shape[2], rows, cols)

def convolve_back(grad, weights, dilation):
    chans, rows, cols = grad.shape
    padded = pad_map(grad)
    summed = jnp.zeros((weights.shape[3], rows * cols), jnp.float32)
    for vertical in range(3):
        for lateral in range(3):
            portion = window(padded, (1 - vertical) * dilation, (1 - lateral) * dilation, rows, cols)
            summed = summed + jnp.dot(weights[vertical, lateral].T, portion.reshape(chans, rows * cols), preferred_element_type=jnp.float32)
    return summed.reshape(weights.shape[3], rows, cols)

def weight_grad(grad, field, dilation):
    chans, rows, cols = field.shape
    padded = pad_map(field)
    flat = grad.reshape(grad.shape[0], rows * cols)
    blocks = []
    for vertical in range(3):
        across = []
        for lateral in range(3):
            portion = window(padded, (vertical - 1) * dilation, (lateral - 1) * dilation, rows, cols)
            across.append(lax.dot_general(flat, portion.reshape(chans, rows * cols), (((1,), (1,)), ((), ())), preferred_element_type=jnp.float32))
        blocks.append(jnp.stack(across))
    return jnp.stack(blocks)

def normalize(hidden, valid, count, gain, shift):
    center = lax.optimization_barrier(jnp.sum(hidden * valid, axis=(1, 2))) / count
    centered = hidden - center[:, None, None]
    spread = lax.optimization_barrier(jnp.sum(centered * centered * valid, axis=(1, 2))) / count
    inverse = lax.rsqrt(spread + EPSILON)
    normed = centered * inverse[:, None, None]
    return (normed, inverse, normed * gain[:, None, None] + shift[:, None, None])

def norm_back(upstream, normed, inverse, valid, count, gain):
    scaled = upstream * gain[:, None, None]
    first = lax.optimization_barrier(jnp.sum(scaled * valid, axis=(1, 2))) / count
    second = lax.optimization_barrier(jnp.sum(scaled * normed * valid, axis=(1, 2))) / count
    return (valid * inverse[:, None, None] * (scaled - first[:, None, None] - normed * second[:, None, None])).astype(jnp.bfloat16)

def reference(pairs, weights_first, weights_second, gains, shifts, dilations, residue_count, cotangent):
    extent = pairs.shape[1]
    marker = (jnp.arange(extent, dtype=jnp.int32) < residue_count[0]).astype(jnp.float32)
    valid = marker[:, None] * marker[None, :]
    count = residue_count[0].astype(jnp.float32) ** 2
    masked = pairs * valid.astype(jnp.bfloat16)
    first = convolve(masked, weights_first, dilations[0])
    normed_one, inverse_one, level_one = normalize(first, valid, count, gains[0], shifts[0])
    active = (valid * jax.nn.elu(level_one)).astype(jnp.bfloat16)
    second = convolve(active, weights_second, dilations[1])
    normed_two, inverse_two, level_two = normalize(second, valid, count, gains[1], shifts[1])
    before = masked.astype(jnp.float32) + level_two
    final = (valid * jax.nn.elu(before)).astype(jnp.bfloat16)
    mirrored = jnp.swapaxes(final, 1, 2)
    symmetric = ((final.astype(jnp.float32) + mirrored.astype(jnp.float32)) * 0.5).astype(jnp.bfloat16)
    back = (cotangent.astype(jnp.float32) + jnp.swapaxes(cotangent, 1, 2).astype(jnp.float32)) * 0.5
    outer = back * valid * jnp.exp(jnp.minimum(before, 0.0))
    grad_two = norm_back(outer, normed_two, inverse_two, valid, count, gains[1])
    upward = convolve_back(grad_two, weights_second, dilations[1])
    inner = upward * valid * jnp.exp(jnp.minimum(level_one, 0.0))
    grad_one = norm_back(inner, normed_one, inverse_one, valid, count, gains[0])
    grad_pairs = (valid * (outer + convolve_back(grad_one, weights_first, dilations[0]))).astype(jnp.bfloat16)
    grad_weights = jnp.stack([weight_grad(grad_one, masked, dilations[0]), weight_grad(grad_two, active, dilations[1])])
    return (symmetric, grad_pairs, grad_weights)
```

```python
import functools

import jax
import jax.numpy as jnp
from jax import lax
from jax.experimental import pallas as pl
from jax.experimental.pallas import tpu as pltpu
from jax.sharding import PartitionSpec as P

MESH = pl.DeviceIdType.MESH
F32 = jnp.float32
BF16 = jnp.bfloat16
EPSILON = 1e-05
EDGE = 16
PAIRS, ACTIVE, GRAD_TWO, GRAD_ONE = range(4)


def roll(x, shift):
    return pltpu.roll(x, shift, 1)


def kernel(
    R,
    C,
    dil_ref,
    count_ref,
    pairs_ref,
    cot_ref,
    w_first_ref,
    w_second_ref,
    gains_ref,
    shifts_ref,
    sym_ref,
    gp_ref,
    gw_ref,
    pin,
    cin,
    fin_out,
    fin_in,
    gp_out,
    mir_s,
    mir_r,
    ext,
    lat_s,
    lat_r,
    taps,
    S,
    Sb,
    first,
    second,
    slope_one,
    outer,
    inner,
    wmat,
    gain_b,
    shift_b,
    ar_s,
    ar_r,
    w_acc,
    w_parts,
    w_a,
    w_b_s,
    w_b,
    w_c_s,
    w_c,
    tile_send,
    tile_recv,
    halo_send,
    halo_recv,
    mir_send,
    mir_recv,
    ar_send_sem,
    ar_recv_sem,
    w_send_sem,
    w_recv_sem,
):
    CH, RT, CT = 64, 32, 128
    row = lax.axis_index("row")
    col = lax.axis_index("col")
    half = C // 2
    G1, G2 = 2 * C, R // 2
    share = 16 // G1
    m, p = row // 2, (row % 2) * C + col

    def place(tr, tc):
        z = (C - tc) % C
        return 2 * (tr // 2) + z // half, 2 * (z % half) + tr % 2

    def tile_of(r, c):
        z = (r % 2) * half + c // 2
        return 2 * (r // 2) + c % 2, (C - z) % C

    def holder(tr, tc):
        return tr, tc

    lr, lc = tile_of(row, col)
    up, down = (lr + R - 1) % R, (lr + 1) % R
    left, right = (lc + C - 1) % C, (lc + 1) % C

    def is_me(target):
        return jnp.logical_and(target[0] == row, target[1] == col)

    def remote(src, dst, send, recv, target):
        return pltpu.make_async_remote_copy(
            src_ref=src,
            dst_ref=dst,
            send_sem=send,
            recv_sem=recv,
            device_id=target,
            device_id_type=MESH,
        )

    def wait_bytes(ref, sem):
        pltpu.make_async_copy(ref, ref, sem).wait()

    barrier = pltpu.get_barrier_semaphore()

    def greet(target):
        pl.semaphore_signal(barrier, inc=1, device_id=target, device_id_type=MESH)

    def greet_one(k, _):
        t = (p + k) % G1
        greet((2 * m + t // C, t % C))
        return 0

    def greet_two(k, _):
        t = (m + k) % G2
        greet((2 * t + row % 2, col))
        return 0

    lax.fori_loop(1, G1, greet_one, 0)
    lax.fori_loop(1, G2, greet_two, 0)
    across = (lr + R - 1 + 2 * (lr % 2)) % R
    for tc in (left, lc, right):
        greet(place(across, tc))
    expected = G1 - 1 + G2 - 1 + 3
    for b in range(4):
        for target in (place(4 * col + b, row // 4), holder(4 * lc + b, lr // 4)):
            other = jnp.logical_not(is_me(target))
            expected = expected + other.astype(jnp.int32)

            @pl.when(other)
            def _(target=target):
                greet(target)

    n = count_ref[0]
    count = jnp.full((1, CT), 1.0, F32) * (n.astype(F32) * n.astype(F32))
    lane = lax.broadcasted_iota(jnp.int32, (CH, CT), 1)
    lane_row = lax.broadcasted_iota(jnp.int32, (1, CT), 1)
    col_valid = (lane + lc * CT < n).astype(F32)
    lane_block = lane // 16

    def valid_row(i):
        return jnp.where(lr * RT + i < n, col_valid, 0.0)

    for k, ref in enumerate((w_first_ref, w_second_ref)):
        blocks = [ref[a, b] for a in range(3) for b in range(3)]
        wmat[2 * k] = jnp.concatenate(blocks, axis=1)
        flipped = [blocks[8 - t].astype(F32).T.astype(BF16) for t in range(9)]
        wmat[2 * k + 1] = jnp.concatenate(flipped, axis=1)
    for k in range(2):
        gain_b[k] = jnp.broadcast_to(gains_ref[k : k + 1, :], (CT, CH)).T
        shift_b[k] = jnp.broadcast_to(shifts_ref[k : k + 1, :], (CT, CH)).T

    pl.semaphore_wait(barrier, expected)

    def move_tile(k, src, dst, target):
        @pl.when(is_me(target))
        def _():
            pltpu.make_async_copy(src, dst, tile_recv.at[k]).start()

        @pl.when(jnp.logical_not(is_me(target)))
        def _():
            remote(src, dst, tile_send.at[k], tile_recv.at[k], target).start()

    def moved(k, dst):
        wait_bytes(dst, tile_recv.at[k])

    def sent_tile(k, src, target):
        @pl.when(jnp.logical_not(is_me(target)))
        def _():
            wait_bytes(src, tile_send.at[k])

    worker, keeper = place(row, col), holder(lr, lc)
    move_tile(0, pairs_ref, pin, worker)

    def mirror_pack(k, src):
        def step(g, _):
            turned = src[pl.ds(pl.multiple_of(128 * g, 128), 128), :].T
            for b in range(4):
                mir_s[k, b, g] = turned[32 * b : 32 * b + 32].astype(BF16)
            return 0

        lax.fori_loop(0, 16, step, 0)

    def mirror_start(k, tr, tc, where):
        slot = tr % 4
        for b in range(4):
            target = where(4 * tc + b, tr // 4)
            src, dst = mir_s.at[k, b], mir_r.at[k, slot]

            @pl.when(is_me(target))
            def _(src=src, dst=dst):
                pltpu.make_async_copy(src, dst, mir_recv.at[k, slot]).start()

            @pl.when(jnp.logical_not(is_me(target)))
            def _(src=src, dst=dst, target=target, b=b):
                remote(src, dst, mir_send.at[k, b], mir_recv.at[k, slot], target).start()

    def mirror_sent(k, tr, tc, where):
        for b in range(4):
            target = where(4 * tc + b, tr // 4)

            @pl.when(jnp.logical_not(is_me(target)))
            def _(b=b):
                wait_bytes(mir_s.at[k, b], mir_send.at[k, b])

    def mirror_wait(k):
        for s in range(4):
            wait_bytes(mir_r.at[k, s], mir_recv.at[k, s])

    quarter = lax.broadcasted_iota(jnp.int32, (RT, CT), 1) // 32

    def mirror_step(k, g, use):
        got = [mir_r[k, s, g].astype(F32) for s in range(4)]
        for kk in range(4):
            flip = got[kk]
            for s in range(4):
                if s != kk:
                    flip = jnp.where(quarter == s, roll(got[s], (32 * (s - kk)) % 128), flip)
            use(4 * g + kk, flip)

    def to_channels(src, dst):
        def step(g, _):
            block = src[pl.ds(4 * g, 4)].astype(F32).reshape(128, 128)
            dst[pl.ds(pl.multiple_of(128 * g, 128), 128), :] = block
            return 0

        lax.fori_loop(0, 16, step, 0)

    to_channels(cot_ref, S)
    mirror_pack(0, S)

    def keep_rows(ph, value):
        def step(g, _):
            low = jnp.zeros((CH, CT), F32)
            high = jnp.zeros((CH, CT), F32)
            for q in range(8):
                i = 8 * g + q
                v = value(i)
                ext[ph, EDGE + i] = v.astype(BF16)
                here = lane_block == q
                low = jnp.where(here, roll(v, 16 * q) if q else v, low)
                high = jnp.where(here, roll(v, (16 * q + 16) % 128) if q < 7 else v, high)
            lat_s[ph, 0, g] = low.astype(BF16)
            lat_s[ph, 1, g] = high.astype(BF16)
            return 0

        lax.fori_loop(0, 4, step, 0)

    def halo_copies(ph):
        whole, top, bottom = pl.ds(0, 4), pl.ds(0, 2), pl.ds(2, 2)
        mid, head, tail = pl.ds(2, 4), pl.ds(0, 2), pl.ds(6, 2)
        own, got = ext.at[ph], lat_r.at[ph]
        low, high = lat_s.at[ph, 0], lat_s.at[ph, 1]
        plan = (
            (own.at[pl.ds(16, 16)], own.at[pl.ds(48, 16)], (up, lc)),
            (own.at[pl.ds(32, 16)], own.at[pl.ds(0, 16)], (down, lc)),
            (low.at[whole], got.at[1, mid], (lr, left)),
            (high.at[whole], got.at[0, mid], (lr, right)),
            (low.at[top], got.at[1, tail], (up, left)),
            (high.at[top], got.at[0, tail], (up, right)),
            (low.at[bottom], got.at[1, head], (down, left)),
            (high.at[bottom], got.at[0, head], (down, right)),
        )
        return [
            remote(src, dst, halo_send.at[ph, k], halo_recv.at[ph, k], place(*tile))
            for k, (src, dst, tile) in enumerate(plan)
        ]

    def halo_start(ph):
        for copy in halo_copies(ph):
            copy.start()

    def halo_wait(ph):
        for copy in halo_copies(ph):
            copy.wait()
        rows16 = jnp.zeros((EDGE, CH, CT), BF16)
        two = jnp.zeros((2, CH, CT), BF16)
        eight = jnp.zeros((8, CH, CT), BF16)

        @pl.when(lr == 0)
        def _():
            ext[ph, 0:EDGE] = rows16
            lat_r[ph, 0, 0:2] = two
            lat_r[ph, 1, 0:2] = two

        @pl.when(lr == R - 1)
        def _():
            ext[ph, EDGE + RT :] = rows16
            lat_r[ph, 0, 6:8] = two
            lat_r[ph, 1, 6:8] = two

        @pl.when(lc == 0)
        def _():
            lat_r[ph, 0] = eight

        @pl.when(lc == C - 1)
        def _():
            lat_r[ph, 1] = eight

    def spread(ph, d):
        back_by, ahead_by = lane >= d, lane < CT - d

        def step(g, _):
            before = lat_r[ph, 0, g].astype(F32)
            after = lat_r[ph, 1, g].astype(F32)
            for q in range(8):
                e = 8 * g + q
                v = ext[ph, e]
                wide = v.astype(F32)
                low = jnp.where(back_by, roll(wide, d), roll(before, (240 + d - 16 * q) % CT))
                high = jnp.where(ahead_by, roll(wide, CT - d), roll(after, (256 - d - 16 * q) % CT))
                taps[ph, e, 0:CH] = low.astype(BF16)
                taps[ph, e, CH : 2 * CH] = v
                taps[ph, e, 2 * CH :] = high.astype(BF16)
            return 0

        lax.fori_loop(0, 8, step, 0)

    def window(ph, d, i):
        rows = []
        for a in range(3):
            at = i + EDGE + (a - 1) * d
            rows.append(jnp.concatenate([taps[ph, at], taps[ph, at + 1]], axis=1))
        return jnp.concatenate(rows, axis=0)

    def convolve(ph, d, k, use, carry):
        weights = wmat[k]

        def step(t, carry):
            i = 2 * t
            out = jnp.dot(weights, window(ph, d, i), preferred_element_type=F32)
            carry = use(i, out[:, :CT], carry)
            return use(i + 1, out[:, CT:], carry)

        return lax.fori_loop(0, RT // 2, step, carry)

    def to_message(one, two):
        return jnp.sum(jnp.concatenate([one, two], axis=0).T, axis=0, keepdims=True)

    def from_message(msg):
        wide = jnp.broadcast_to(msg, (CT, CT)).T
        return wide[:CH], wide[CH:]

    def sum_start(q, msg):
        mine = m if q % 2 else p
        size = G2 if q % 2 else G1
        ar_s[q] = msg
        ar_r[q, mine] = msg

        def step(k, _):
            t = (mine + k) % size
            target = (2 * t + row % 2, col) if q % 2 else (2 * m + t // C, t % C)
            remote(ar_s.at[q], ar_r.at[q, mine], ar_send_sem.at[q], ar_recv_sem.at[q], target).start()
            return 0

        lax.fori_loop(1, size, step, 0)

    def sum_wait(q):
        size = G2 if q % 2 else G1
        wait_bytes(ar_r.at[q, pl.ds(0, size - 1)], ar_recv_sem.at[q])
        return [ar_r[q, t] for t in range(size)]

    def plain(parts):
        total = parts[0]
        for part in parts[1:]:
            total = total + part
        return total

    def wide_count(number):
        return jnp.full((1, CT), 1.0, F32) * number.astype(F32)

    def pooled(parts, numbers):
        counts = [wide_count(number) for number in numbers]
        total = plain(parts)
        mean = total / jnp.maximum(plain(counts), 1.0)
        apart = jnp.zeros((1, CT), F32)
        for part, number in zip(parts, counts):
            off = part / jnp.maximum(number, 1.0) - mean
            apart = apart + number * off * off
        return jnp.where(lane_row < CH, total, total + roll(apart, CH))

    def extent(start, size):
        return jnp.clip(n - start, 0, size)

    def tile_count(tr, tc):
        return extent(tr * RT, RT) * extent(tc * CT, CT)

    def sums(q):
        sum_start(q + 1, plain(sum_wait(q)))
        return plain(sum_wait(q + 1))

    def norm(q, field, total):
        own = wide_count(tile_count(lr, lc))
        center = jnp.sum(total, axis=1, keepdims=True) / jnp.maximum(own, 1.0)

        def step(i, acc):
            off = (field[i] - center) * valid_row(i)
            return acc + off * off

        spread_sum = lax.fori_loop(0, RT, step, jnp.zeros((CH, CT), F32), unroll=4)
        sum_start(q, to_message(total, spread_sum))
        parts = sum_wait(q)
        numbers = [tile_count(*tile_of(2 * m + t // C, t % C)) for t in range(G1)]
        sum_start(q + 1, pooled(parts, numbers))
        parts = sum_wait(q + 1)
        numbers = [extent(2 * RT * t, 2 * RT) * n for t in range(G2)]
        mean, var = from_message(pooled(parts, numbers) / count)
        return mean, lax.rsqrt(var + EPSILON)

    def grad_taps(k, ph, d, grads):
        w_acc[...] = jnp.zeros(w_acc.shape, F32)

        def step(t, _):
            i = 2 * t
            g = jnp.concatenate([ext[grads, EDGE + i], ext[grads, EDGE + i + 1]], axis=1)
            w_acc[:, : 9 * CH] += lax.dot_general(
                g, window(ph, d, i), (((1,), (1,)), ((), ())), preferred_element_type=F32
            )
            return 0

        lax.fori_loop(0, RT // 2, step, 0)
        for t in range(16):
            r, c = 8 * (t // 2), 384 * (t % 2)
            w_parts[k, t // share, t % share] = w_acc[r : r + 8, c : c + 384]
        w_a[k, p] = w_parts[k, p]

        def send(j, _):
            t = (p + j) % G1
            remote(
                w_parts.at[k, t], w_a.at[k, p], w_send_sem.at[k, 0], w_recv_sem.at[k, 0],
                (2 * m + t // C, t % C),
            ).start()
            return 0

        lax.fori_loop(1, G1, send, 0)

    def grad_taps_across(k):
        wait_bytes(w_a.at[k, pl.ds(0, G1 - 1)], w_recv_sem.at[k, 0])
        total = plain([w_a[k, t] for t in range(G1)])
        w_b_s[k] = total
        w_b[k, m] = total

        def send(j, _):
            t = (m + j) % G2
            remote(
                w_b_s.at[k], w_b.at[k, m], w_send_sem.at[k, 1], w_recv_sem.at[k, 1],
                (2 * t + row % 2, col),
            ).start()
            return 0

        lax.fori_loop(1, G2, send, 0)

    def grad_taps_back(k):
        wait_bytes(w_b.at[k, pl.ds(0, G2 - 1)], w_recv_sem.at[k, 1])
        total = plain([w_b[k, t] for t in range(G2)])
        w_c_s[k] = total
        w_c[k, p] = total

        def send(j, _):
            t = (p + j) % G1
            remote(
                w_c_s.at[k], w_c.at[k, p], w_send_sem.at[k, 2], w_recv_sem.at[k, 2],
                (2 * m + t // C, t % C),
            ).start()
            return 0

        lax.fori_loop(1, G1, send, 0)

    def grad_taps_end(k):
        wait_bytes(w_c.at[k, pl.ds(0, G1 - 1)], w_recv_sem.at[k, 2])
        for t in range(16):
            r, c = 8 * (t // 2), 384 * (t % 2)
            part = w_c[k, t // share, t % share]
            for tap in range(9):
                at = CH * tap - c
                if 0 <= at < 384:
                    gw_ref[k, tap // 3, tap % 3, r : r + 8, :] = part[:, at : at + CH]

    d_one, d_two = dil_ref[0], dil_ref[1]
    moved(0, pin)
    to_channels(pin, S)
    keep_rows(PAIRS, lambda i: S[pl.ds(i, CH, stride=RT), :] * valid_row(i))
    halo_start(PAIRS)
    halo_wait(PAIRS)
    move_tile(1, cot_ref, cin, worker)
    mirror_start(0, row, col, place)
    spread(PAIRS, d_one)

    def keep(field):
        def use(i, out, total):
            field[i] = out
            return total + out * valid_row(i)

        return use

    nothing = jnp.zeros((CH, CT), F32)
    total = convolve(PAIRS, d_one, 0, keep(first), nothing)
    mean_one, inv_one = norm(0, first, total)
    scale_one = inv_one * gain_b[0]
    shift_one = shift_b[0]

    def activate(i):
        level = (first[i] - mean_one) * scale_one + shift_one
        low = jnp.exp(jnp.minimum(level, 0.0))
        valid = valid_row(i)
        slope_one[i] = low * valid
        return jnp.where(level > 0.0, level, low - 1.0) * valid

    keep_rows(ACTIVE, activate)
    halo_start(ACTIVE)

    halo_wait(ACTIVE)
    spread(ACTIVE, d_two)
    total = convolve(ACTIVE, d_two, 2, keep(second), nothing)
    mean_two, inv_two = norm(2, second, total)
    moved(1, cin)
    mirror_wait(0)

    def join_cotangent(g, _):
        def use(c, flip):
            back = (cin[c].astype(F32) + flip) * 0.5
            Sb[pl.ds(pl.multiple_of(RT * c, RT), RT), :] = back

        mirror_step(0, g, use)
        return 0

    lax.fori_loop(0, 16, join_cotangent, 0)
    gain_two = gain_b[1]
    scale_two = inv_two * gain_two
    shift_two = shift_b[1]

    def finish(i, carry):
        p_sum, q_sum = carry
        off = second[i] - mean_two
        before = ext[PAIRS, EDGE + i].astype(F32) + (off * scale_two + shift_two)
        low = jnp.exp(jnp.minimum(before, 0.0))
        valid = valid_row(i)
        S[pl.ds(i, CH, stride=RT), :] = jnp.where(before > 0.0, before, low - 1.0) * valid
        out = Sb[pl.ds(i, CH, stride=RT), :] * valid * low
        outer[i] = out
        scaled = out * gain_two
        return p_sum + scaled, q_sum + scaled * (off * inv_two)

    p_sum, q_sum = lax.fori_loop(0, RT, finish, (nothing, nothing))
    sum_start(4, to_message(p_sum, q_sum))

    def keep_final(g, _):
        block = S[pl.ds(pl.multiple_of(128 * g, 128), 128), :]
        fin_out[pl.ds(4 * g, 4)] = block.reshape(4, RT, CT).astype(BF16)
        return 0

    lax.fori_loop(0, 16, keep_final, 0)
    mirror_pack(1, S)

    p_two, q_two = from_message(sums(4) / count)

    def back_two(i):
        normed = (second[i] - mean_two) * inv_two
        scaled = outer[i] * gain_two
        return valid_row(i) * inv_two * (scaled - p_two - normed * q_two)

    keep_rows(GRAD_TWO, back_two)
    halo_start(GRAD_TWO)
    grad_taps(1, ACTIVE, d_two, GRAD_TWO)
    halo_wait(GRAD_TWO)
    move_tile(2, fin_out, fin_in, keeper)
    mirror_start(1, lr, lc, holder)
    spread(GRAD_TWO, d_two)
    gain_one = gain_b[0]

    def descend(i, out, carry):
        p_sum, q_sum = carry
        up_i = out * slope_one[i]
        inner[i] = up_i
        scaled = up_i * gain_one
        return p_sum + scaled, q_sum + scaled * ((first[i] - mean_one) * inv_one)

    p_sum, q_sum = convolve(GRAD_TWO, d_two, 3, descend, (nothing, nothing))
    sum_start(6, to_message(p_sum, q_sum))
    grad_taps_across(1)
    p_one, q_one = from_message(sums(6) / count)

    def back_one(i):
        normed = (first[i] - mean_one) * inv_one
        scaled = inner[i] * gain_one
        return valid_row(i) * inv_one * (scaled - p_one - normed * q_one)

    keep_rows(GRAD_ONE, back_one)
    halo_start(GRAD_ONE)
    grad_taps(0, PAIRS, d_one, GRAD_ONE)
    grad_taps_back(1)
    halo_wait(GRAD_ONE)
    spread(GRAD_ONE, d_one)

    def lower(i, out, carry):
        S[pl.ds(i, CH, stride=RT), :] = (outer[i] + out) * valid_row(i)
        return carry

    convolve(GRAD_ONE, d_one, 1, lower, 0)

    def keep_grad(g, _):
        block = S[pl.ds(pl.multiple_of(128 * g, 128), 128), :]
        gp_out[pl.ds(4 * g, 4)] = block.reshape(4, RT, CT).astype(BF16)
        return 0

    lax.fori_loop(0, 16, keep_grad, 0)
    move_tile(3, gp_out, gp_ref, keeper)
    grad_taps_across(0)
    moved(2, fin_in)
    mirror_wait(1)

    def join_final(g, _):
        def use(c, flip):
            sym_ref[c] = ((fin_in[c].astype(F32) + flip) * 0.5).astype(BF16)

        mirror_step(1, g, use)
        return 0

    lax.fori_loop(0, 16, join_final, 0)
    grad_taps_back(0)
    grad_taps_end(1)
    grad_taps_end(0)

    sent_tile(0, pin, worker)
    sent_tile(1, cin, worker)
    sent_tile(2, fin_out, keeper)
    sent_tile(3, gp_out, keeper)
    mirror_sent(0, row, col, place)
    mirror_sent(1, lr, lc, holder)
    for q in range(8):
        size = G2 if q % 2 else G1
        wait_bytes(ar_r.at[q, pl.ds(0, size - 1)], ar_send_sem.at[q])
    for k in range(2):
        wait_bytes(w_a.at[k, pl.ds(0, G1 - 1)], w_send_sem.at[k, 0])
        wait_bytes(w_b.at[k, pl.ds(0, G2 - 1)], w_send_sem.at[k, 1])
        wait_bytes(w_c.at[k, pl.ds(0, G1 - 1)], w_send_sem.at[k, 2])
    moved(3, gp_out)


def solution(mesh):
    R, C = mesh.shape["row"], mesh.shape["col"]

    def per_device(pairs, w_first, w_second, gains, shifts, dilations, residue_count, cotangent):
        CH, RT, CT = pairs.shape
        G1, G2 = 2 * C, R // 2
        G, share = max(G1, G2), 16 // G1
        vmem = pl.BlockSpec(memory_space=pltpu.VMEM)
        smem = pl.BlockSpec(memory_space=pltpu.SMEM)
        anywhere = pl.BlockSpec(memory_space=pl.ANY)
        tile = pltpu.VMEM((CH, RT, CT), BF16)
        field = pltpu.VMEM((RT, CH, CT), F32)
        flat = pltpu.VMEM((CH * RT, CT), F32)
        dma = pltpu.SemaphoreType.DMA
        return pl.pallas_call(
            functools.partial(kernel, R, C),
            out_shape=(
                jax.ShapeDtypeStruct((CH, RT, CT), BF16),
                jax.ShapeDtypeStruct((CH, RT, CT), BF16),
                jax.ShapeDtypeStruct((2, 3, 3, CH, CH), F32),
            ),
            in_specs=[smem, smem, anywhere, vmem, vmem, vmem, vmem, vmem],
            out_specs=(vmem, anywhere, vmem),
            scratch_shapes=[
                tile,
                tile,
                tile,
                tile,
                tile,
                pltpu.VMEM((2, 4, 16, RT, CT), BF16),
                pltpu.VMEM((2, 4, 16, RT, CT), BF16),
                pltpu.VMEM((4, RT + 2 * EDGE, CH, CT), BF16),
                pltpu.VMEM((4, 2, 4, CH, CT), BF16),
                pltpu.VMEM((4, 2, 8, CH, CT), BF16),
                pltpu.VMEM((4, RT + 2 * EDGE, 3 * CH, CT), BF16),
                flat,
                flat,
                field,
                field,
                field,
                field,
                field,
                pltpu.VMEM((4, CH, 9 * CH), BF16),
                pltpu.VMEM((2, CH, CT), F32),
                pltpu.VMEM((2, CH, CT), F32),
                pltpu.VMEM((8, 1, CT), F32),
                pltpu.VMEM((8, G, 1, CT), F32),
                pltpu.VMEM((CH, 768), F32),
                pltpu.VMEM((2, G1, share, 8, 384), F32),
                pltpu.VMEM((2, G1, share, 8, 384), F32),
                pltpu.VMEM((2, share, 8, 384), F32),
                pltpu.VMEM((2, G2, share, 8, 384), F32),
                pltpu.VMEM((2, share, 8, 384), F32),
                pltpu.VMEM((2, G1, share, 8, 384), F32),
                dma((4,)),
                dma((4,)),
                dma((4, 8)),
                dma((4, 8)),
                dma((2, 4)),
                dma((2, 4)),
                dma((8,)),
                dma((8,)),
                dma((2, 3)),
                dma((2, 3)),
            ],
            compiler_params=pltpu.CompilerParams(
                collective_id=0, has_side_effects=True, vmem_limit_bytes=56 * 1024 * 1024
            ),
            cost_estimate=pl.CostEstimate(
                flops=6 * 2 * 9 * CH * CH * RT * CT, bytes_accessed=4 * CH * RT * CT, transcendentals=0
            ),
        )(dilations, residue_count, pairs, cotangent, w_first, w_second, gains, shifts)

    in_specs = (P(None, "row", "col"), P(), P(), P(), P(), P(), P(), P(None, "row", "col"))
    out_specs = (P(None, "row", "col"), P(None, "row", "col"), P())
    return jax.shard_map(
        per_device, mesh=mesh, in_specs=in_specs, out_specs=out_specs, check_vma=False
    )
```

```python
import functools

import jax
import jax.numpy as jnp
from jax import lax
from jax.experimental import pallas as pl
from jax.experimental.pallas import tpu as pltpu
from jax.sharding import PartitionSpec as P

MESH = pl.DeviceIdType.MESH
F32 = jnp.float32
BF16 = jnp.bfloat16
EPSILON = 1e-05
EDGE = 16
PAIRS, ACTIVE, GRAD_TWO, GRAD_ONE = range(4)
CHIPS = (2, 7, 6, 4, 3, 1, 0, 5)


def roll(x, shift):
    return pltpu.roll(x, shift, 1)


def kernel(
    R,
    C,
    dil_ref,
    count_ref,
    pairs_ref,
    cot_ref,
    w_first_ref,
    w_second_ref,
    gains_ref,
    shifts_ref,
    sym_ref,
    gp_ref,
    gw_ref,
    pin,
    cin,
    fin_out,
    fin_in,
    gp_out,
    mir_s,
    mir_r,
    relayed,
    ext,
    lat_s,
    lat_r,
    taps,
    S,
    Sb,
    first,
    second,
    slope_one,
    outer,
    inner,
    wmat,
    gain_b,
    shift_b,
    ar_s,
    ar_r,
    w_acc,
    w_parts,
    w_a,
    w_b_s,
    w_b,
    w_c_s,
    w_c,
    tile_send,
    tile_recv,
    halo_send,
    halo_recv,
    mir_send,
    mir_recv,
    ar_send_sem,
    ar_recv_sem,
    relay_send,
    relay_recv,
    w_send_sem,
    w_recv_sem,
):
    CH, RT, CT = 64, 32, 128
    row = lax.axis_index("row")
    col = lax.axis_index("col")
    half = C // 2
    G1, G2 = 2 * C, R // 2
    share = 16 // G1
    m, p = row // 2, (row % 2) * C + col

    chips = CHIPS if C == len(CHIPS) else tuple(range(C))

    def pick(table, k):
        found = jnp.int32(0)
        for j, entry in enumerate(table):
            found = found + jnp.where(k == j, entry, 0)
        return found

    def place(tr, tc):
        z = pick(chips, tc)
        return 2 * (tr // 2) + z // half, 2 * (z % half) + tr % 2

    def tile_of(r, c):
        z = (r % 2) * half + c // 2
        return 2 * (r // 2) + c % 2, pick([chips.index(j) for j in range(C)], z)

    def holder(tr, tc):
        return tr, tc

    lr, lc = tile_of(row, col)
    up, down = (lr + R - 1) % R, (lr + 1) % R
    left, right = (lc + C - 1) % C, (lc + 1) % C

    def is_me(target):
        return jnp.logical_and(target[0] == row, target[1] == col)

    def remote(src, dst, send, recv, target):
        return pltpu.make_async_remote_copy(
            src_ref=src,
            dst_ref=dst,
            send_sem=send,
            recv_sem=recv,
            device_id=target,
            device_id_type=MESH,
        )

    def wait_bytes(ref, sem):
        pltpu.make_async_copy(ref, ref, sem).wait()

    barrier = pltpu.get_barrier_semaphore()

    def greet(target):
        pl.semaphore_signal(barrier, inc=1, device_id=target, device_id_type=MESH)

    def greet_one(k, _):
        t = (p + k) % G1
        greet((2 * m + t // C, t % C))
        return 0

    def greet_two(k, _):
        t = (m + k) % G2
        greet((2 * t + row % 2, col))
        return 0

    lax.fori_loop(1, G1, greet_one, 0)
    lax.fori_loop(1, G2, greet_two, 0)
    across = (lr + R - 1 + 2 * (lr % 2)) % R
    for tc in (left, lc, right):
        greet(place(across, tc))
    expected = G1 - 1 + G2 - 1 + 3
    relays = m // 4 == col // 2

    def relay_of(b):
        mt = 2 * col + b // 2
        return 2 * mt + row % 2, 2 * (col // 2) + b % 2

    for b in range(4):
        expected = expected + jnp.logical_not(is_me(relay_of(b))).astype(jnp.int32)

    def greet_source(j, _):
        source = (2 * j + row % 2, m // 2)

        @pl.when(jnp.logical_and(relays, jnp.logical_not(is_me(source))))
        def _():
            greet(source)

        return 0

    lax.fori_loop(0, G2, greet_source, 0)

    n = count_ref[0]
    count = jnp.full((1, CT), 1.0, F32) * (n.astype(F32) * n.astype(F32))
    lane = lax.broadcasted_iota(jnp.int32, (CH, CT), 1)
    lane_row = lax.broadcasted_iota(jnp.int32, (1, CT), 1)
    col_valid = (lane + lc * CT < n).astype(F32)
    lane_block = lane // 16

    def valid_row(i):
        return jnp.where(lr * RT + i < n, col_valid, 0.0)

    for k, ref in enumerate((w_first_ref, w_second_ref)):
        blocks = [ref[a, b] for a in range(3) for b in range(3)]
        wmat[2 * k] = jnp.concatenate(blocks, axis=1)
        flipped = [blocks[8 - t].astype(F32).T.astype(BF16) for t in range(9)]
        wmat[2 * k + 1] = jnp.concatenate(flipped, axis=1)
    for k in range(2):
        gain_b[k] = jnp.broadcast_to(gains_ref[k : k + 1, :], (CT, CH)).T
        shift_b[k] = jnp.broadcast_to(shifts_ref[k : k + 1, :], (CT, CH)).T

    def move_tile(k, src, dst, target):
        either(src, dst, tile_send.at[k], tile_recv.at[k], target)

    def moved(k, dst):
        wait_bytes(dst, tile_recv.at[k])

    def sent_tile(k, src, target):
        @pl.when(jnp.logical_not(is_me(target)))
        def _():
            wait_bytes(src, tile_send.at[k])

    worker, keeper = place(row, col), holder(lr, lc)
    lower_half, upper_half = pl.ds(0, CH // 2), pl.ds(CH // 2, CH // 2)

    def mirror_pack(k, src):
        def step(g, _):
            turned = src[pl.ds(pl.multiple_of(128 * g, 128), 128), :].T
            for b in range(4):
                mir_s[k, b, g] = turned[32 * b : 32 * b + 32].astype(BF16)
            return 0

        lax.fori_loop(0, 16, step, 0)

    def either(src, dst, send, recv, target):
        @pl.when(is_me(target))
        def _():
            pltpu.make_async_copy(src, dst, recv).start()

        @pl.when(jnp.logical_not(is_me(target)))
        def _():
            remote(src, dst, send, recv, target).start()

    def cross_start():
        for b in range(4):
            either(mir_s.at[0, b], relayed.at[m], mir_send.at[0, b], relay_recv.at[m], relay_of(b))

    def cross_target(j):
        return place(2 * m + col % 2, j // 2)

    def cross_on(first, last):
        def step(j, _):
            @pl.when(relays)
            def _():
                wait_bytes(relayed.at[j], relay_recv.at[j])
                slot = 2 * (j % 2) + row % 2
                either(
                    relayed.at[j], mir_r.at[0, slot], relay_send.at[j], mir_recv.at[0, slot], cross_target(j)
                )

            return 0

        lax.fori_loop(first, last, step, 0)

    def cross_sent():
        for b in range(4):

            @pl.when(jnp.logical_not(is_me(relay_of(b))))
            def _(b=b):
                wait_bytes(mir_s.at[0, b], mir_send.at[0, b])

        def step(j, _):
            @pl.when(jnp.logical_and(relays, jnp.logical_not(is_me(cross_target(j)))))
            def _():
                wait_bytes(relayed.at[j], relay_send.at[j])

            return 0

        lax.fori_loop(0, G2, step, 0)

    def mirror_block(b):
        either(
            mir_s.at[1, b], mir_r.at[1, lr % 4], mir_send.at[1, b], mir_recv.at[1, lr % 4],
            holder(4 * lc + b, lr // 4),
        )

    def mirror_sent():
        for b in range(4):

            @pl.when(jnp.logical_not(is_me(holder(4 * lc + b, lr // 4))))
            def _(b=b):
                wait_bytes(mir_s.at[1, b], mir_send.at[1, b])

    def mirror_wait(k):
        for s in range(4):
            wait_bytes(mir_r.at[k, s], mir_recv.at[k, s])

    quarter = lax.broadcasted_iota(jnp.int32, (RT, CT), 1) // 32

    def mirror_step(k, g, use):
        got = [mir_r[k, s, g].astype(F32) for s in range(4)]
        for kk in range(4):
            flip = got[kk]
            for s in range(4):
                if s != kk:
                    flip = jnp.where(quarter == s, roll(got[s], (32 * (s - kk)) % 128), flip)
            use(4 * g + kk, flip)

    def to_channels(src, dst):
        def step(g, _):
            block = src[pl.ds(4 * g, 4)].astype(F32).reshape(128, 128)
            dst[pl.ds(pl.multiple_of(128 * g, 128), 128), :] = block
            return 0

        lax.fori_loop(0, 16, step, 0)

    to_channels(cot_ref, S)
    mirror_pack(0, S)
    pl.semaphore_wait(barrier, expected)
    move_tile(0, pairs_ref, pin, worker)
    cross_start()

    def keep_rows(ph, value):
        def step(g, _):
            low = jnp.zeros((CH, CT), F32)
            high = jnp.zeros((CH, CT), F32)
            for q in range(8):
                i = 8 * g + q
                v = value(i)
                ext[ph, EDGE + i] = v.astype(BF16)
                here = lane_block == q
                low = jnp.where(here, roll(v, 16 * q) if q else v, low)
                high = jnp.where(here, roll(v, (16 * q + 16) % 128) if q < 7 else v, high)
            lat_s[ph, 0, g] = low.astype(BF16)
            lat_s[ph, 1, g] = high.astype(BF16)
            return 0

        lax.fori_loop(0, 4, step, 0)

    def halo_copies(ph):
        whole, top, bottom = pl.ds(0, 4), pl.ds(0, 2), pl.ds(2, 2)
        mid, head, tail = pl.ds(2, 4), pl.ds(0, 2), pl.ds(6, 2)
        own, got = ext.at[ph], lat_r.at[ph]
        low, high = lat_s.at[ph, 0], lat_s.at[ph, 1]
        plan = (
            (own.at[pl.ds(16, 16)], own.at[pl.ds(48, 16)], (up, lc)),
            (own.at[pl.ds(32, 16)], own.at[pl.ds(0, 16)], (down, lc)),
            (low.at[whole], got.at[1, mid], (lr, left)),
            (high.at[whole], got.at[0, mid], (lr, right)),
            (low.at[top], got.at[1, tail], (up, left)),
            (high.at[top], got.at[0, tail], (up, right)),
            (low.at[bottom], got.at[1, head], (down, left)),
            (high.at[bottom], got.at[0, head], (down, right)),
        )
        return [
            remote(src, dst, halo_send.at[ph, k], halo_recv.at[ph, k], place(*tile))
            for k, (src, dst, tile) in enumerate(plan)
        ]

    def halo_start(ph):
        for copy in halo_copies(ph):
            copy.start()

    def halo_wait(ph):
        for copy in halo_copies(ph):
            copy.wait()
        rows16 = jnp.zeros((EDGE, CH, CT), BF16)
        two = jnp.zeros((2, CH, CT), BF16)
        eight = jnp.zeros((8, CH, CT), BF16)

        @pl.when(lr == 0)
        def _():
            ext[ph, 0:EDGE] = rows16
            lat_r[ph, 0, 0:2] = two
            lat_r[ph, 1, 0:2] = two

        @pl.when(lr == R - 1)
        def _():
            ext[ph, EDGE + RT :] = rows16
            lat_r[ph, 0, 6:8] = two
            lat_r[ph, 1, 6:8] = two

        @pl.when(lc == 0)
        def _():
            lat_r[ph, 0] = eight

        @pl.when(lc == C - 1)
        def _():
            lat_r[ph, 1] = eight

    def spread(ph, d):
        back_by, ahead_by = lane >= d, lane < CT - d

        def step(g, _):
            before = lat_r[ph, 0, g].astype(F32)
            after = lat_r[ph, 1, g].astype(F32)
            for q in range(8):
                e = 8 * g + q
                v = ext[ph, e]
                wide = v.astype(F32)
                low = jnp.where(back_by, roll(wide, d), roll(before, (240 + d - 16 * q) % CT))
                high = jnp.where(ahead_by, roll(wide, CT - d), roll(after, (256 - d - 16 * q) % CT))
                taps[ph, e, 0:CH] = low.astype(BF16)
                taps[ph, e, CH : 2 * CH] = v
                taps[ph, e, 2 * CH :] = high.astype(BF16)
            return 0

        lax.fori_loop(0, 8, step, 0)

    def window(ph, d, i):
        rows = []
        for a in range(3):
            at = i + EDGE + (a - 1) * d
            rows.append(jnp.concatenate([taps[ph, at], taps[ph, at + 1]], axis=1))
        return jnp.concatenate(rows, axis=0)

    def convolve(ph, d, k, use, carry):
        weights = wmat[k]

        def step(t, carry):
            i = 2 * t
            out = jnp.dot(weights, window(ph, d, i), preferred_element_type=F32)
            carry = use(i, out[:, :CT], carry)
            return use(i + 1, out[:, CT:], carry)

        return lax.fori_loop(0, RT // 2, step, carry)

    def to_message(one, two):
        return jnp.sum(jnp.concatenate([one, two], axis=0).T, axis=0, keepdims=True)

    def from_message(msg):
        wide = jnp.broadcast_to(msg, (CT, CT)).T
        return wide[:CH], wide[CH:]

    def sum_start(q, msg):
        mine = m if q % 2 else p
        size = G2 if q % 2 else G1
        ar_s[q] = msg
        ar_r[q, mine] = msg

        def step(k, _):
            t = (mine + k) % size
            target = (2 * t + row % 2, col) if q % 2 else (2 * m + t // C, t % C)
            remote(ar_s.at[q], ar_r.at[q, mine], ar_send_sem.at[q], ar_recv_sem.at[q], target).start()
            return 0

        lax.fori_loop(1, size, step, 0)

    def sum_wait(q):
        size = G2 if q % 2 else G1
        wait_bytes(ar_r.at[q, pl.ds(0, size - 1)], ar_recv_sem.at[q])
        return [ar_r[q, t] for t in range(size)]

    def plain(parts):
        total = parts[0]
        for part in parts[1:]:
            total = total + part
        return total

    def wide_count(number):
        return jnp.full((1, CT), 1.0, F32) * number.astype(F32)

    def pooled(parts, numbers):
        counts = [wide_count(number) for number in numbers]
        total = plain(parts)
        mean = total / jnp.maximum(plain(counts), 1.0)
        apart = jnp.zeros((1, CT), F32)
        for part, number in zip(parts, counts):
            off = part / jnp.maximum(number, 1.0) - mean
            apart = apart + number * off * off
        return jnp.where(lane_row < CH, total, total + roll(apart, CH))

    def extent(start, size):
        return jnp.clip(n - start, 0, size)

    def tile_count(tr, tc):
        return extent(tr * RT, RT) * extent(tc * CT, CT)

    def sums(q, message, beside_one, beside_two):
        sum_start(q, message)
        beside_one()
        sum_start(q + 1, plain(sum_wait(q)))
        beside_two()
        return plain(sum_wait(q + 1))

    def norm(q, field, total, beside_one, beside_two):
        own = wide_count(tile_count(lr, lc))
        center = jnp.sum(total, axis=1, keepdims=True) / jnp.maximum(own, 1.0)

        def step(i, acc):
            off = (field[i] - center) * valid_row(i)
            return acc + off * off

        spread_sum = lax.fori_loop(0, RT, step, jnp.zeros((CH, CT), F32), unroll=4)
        sum_start(q, to_message(total, spread_sum))
        beside_one()
        parts = sum_wait(q)
        numbers = [tile_count(*tile_of(2 * m + t // C, t % C)) for t in range(G1)]
        sum_start(q + 1, pooled(parts, numbers))
        beside_two()
        parts = sum_wait(q + 1)
        numbers = [extent(2 * RT * t, 2 * RT) * n for t in range(G2)]
        mean, var = from_message(pooled(parts, numbers) / count)
        return mean, lax.rsqrt(var + EPSILON)

    def grad_taps(k, ph, d, grads):
        w_acc[...] = jnp.zeros(w_acc.shape, F32)

        def step(t, _):
            i = 2 * t
            g = jnp.concatenate([ext[grads, EDGE + i], ext[grads, EDGE + i + 1]], axis=1)
            w_acc[:, : 9 * CH] += lax.dot_general(
                g, window(ph, d, i), (((1,), (1,)), ((), ())), preferred_element_type=F32
            )
            return 0

        lax.fori_loop(0, RT // 2, step, 0)
        for t in range(16):
            r, c = 8 * (t // 2), 384 * (t % 2)
            w_parts[k, t // share, t % share] = w_acc[r : r + 8, c : c + 384]
        w_a[k, p] = w_parts[k, p]

        def send(j, _):
            t = (p + j) % G1
            remote(
                w_parts.at[k, t], w_a.at[k, p], w_send_sem.at[k, 0], w_recv_sem.at[k, 0],
                (2 * m + t // C, t % C),
            ).start()
            return 0

        lax.fori_loop(1, G1, send, 0)

    def grad_taps_across(k):
        wait_bytes(w_a.at[k, pl.ds(0, G1 - 1)], w_recv_sem.at[k, 0])
        total = plain([w_a[k, t] for t in range(G1)])
        w_b_s[k] = total
        w_b[k, m] = total

        def send(j, _):
            t = (m + j) % G2
            remote(
                w_b_s.at[k], w_b.at[k, m], w_send_sem.at[k, 1], w_recv_sem.at[k, 1],
                (2 * t + row % 2, col),
            ).start()
            return 0

        lax.fori_loop(1, G2, send, 0)

    def grad_taps_back(k):
        wait_bytes(w_b.at[k, pl.ds(0, G2 - 1)], w_recv_sem.at[k, 1])
        total = plain([w_b[k, t] for t in range(G2)])
        w_c_s[k] = total
        w_c[k, p] = total

        def send(j, _):
            t = (p + j) % G1
            remote(
                w_c_s.at[k], w_c.at[k, p], w_send_sem.at[k, 2], w_recv_sem.at[k, 2],
                (2 * m + t // C, t % C),
            ).start()
            return 0

        lax.fori_loop(1, G1, send, 0)

    def grad_taps_end(k):
        wait_bytes(w_c.at[k, pl.ds(0, G1 - 1)], w_recv_sem.at[k, 2])
        for t in range(16):
            r, c = 8 * (t // 2), 384 * (t % 2)
            part = w_c[k, t // share, t % share]
            for tap in range(9):
                at = CH * tap - c
                if 0 <= at < 384:
                    gw_ref[k, tap // 3, tap % 3, r : r + 8, :] = part[:, at : at + CH]

    d_one, d_two = dil_ref[0], dil_ref[1]
    moved(0, pin)
    to_channels(pin, S)
    keep_rows(PAIRS, lambda i: S[pl.ds(i, CH, stride=RT), :] * valid_row(i))
    halo_start(PAIRS)
    move_tile(1, cot_ref, cin, worker)
    halo_wait(PAIRS)
    spread(PAIRS, d_one)

    def keep(field):
        def use(i, out, total):
            field[i] = out
            return total + out * valid_row(i)

        return use

    nothing = jnp.zeros((CH, CT), F32)
    total = convolve(PAIRS, d_one, 0, keep(first), nothing)
    mean_one, inv_one = norm(
        0, first, total, lambda: cross_on(0, G2 // 2), lambda: cross_on(G2 // 2, G2)
    )
    scale_one = inv_one * gain_b[0]
    shift_one = shift_b[0]

    def activate(i):
        level = (first[i] - mean_one) * scale_one + shift_one
        low = jnp.exp(jnp.minimum(level, 0.0))
        valid = valid_row(i)
        slope_one[i] = low * valid
        return jnp.where(level > 0.0, level, low - 1.0) * valid

    keep_rows(ACTIVE, activate)
    halo_start(ACTIVE)

    halo_wait(ACTIVE)
    spread(ACTIVE, d_two)
    total = convolve(ACTIVE, d_two, 2, keep(second), nothing)
    mean_two, inv_two = norm(2, second, total, lambda: None, lambda: None)
    moved(1, cin)
    mirror_wait(0)

    def join_cotangent(g, _):
        def use(c, flip):
            back = (cin[c].astype(F32) + flip) * 0.5
            Sb[pl.ds(pl.multiple_of(RT * c, RT), RT), :] = back

        mirror_step(0, g, use)
        return 0

    lax.fori_loop(0, 16, join_cotangent, 0)
    gain_two = gain_b[1]
    scale_two = inv_two * gain_two
    shift_two = shift_b[1]

    def finish(i, carry):
        p_sum, q_sum = carry
        off = second[i] - mean_two
        before = ext[PAIRS, EDGE + i].astype(F32) + (off * scale_two + shift_two)
        low = jnp.exp(jnp.minimum(before, 0.0))
        valid = valid_row(i)
        S[pl.ds(i, CH, stride=RT), :] = jnp.where(before > 0.0, before, low - 1.0) * valid
        out = Sb[pl.ds(i, CH, stride=RT), :] * valid * low
        outer[i] = out
        scaled = out * gain_two
        return p_sum + scaled, q_sum + scaled * (off * inv_two)

    p_sum, q_sum = lax.fori_loop(0, RT, finish, (nothing, nothing))

    def send_final():
        def keep_final(g, _):
            block = S[pl.ds(pl.multiple_of(128 * g, 128), 128), :]
            fin_out[pl.ds(4 * g, 4)] = block.reshape(4, RT, CT).astype(BF16)
            return 0

        lax.fori_loop(0, 16, keep_final, 0)
        move_tile(2, fin_out.at[lower_half], fin_in.at[lower_half], keeper)
        mirror_pack(1, S)

    def send_final_rest():
        move_tile(3, fin_out.at[upper_half], fin_in.at[upper_half], keeper)

    totals = sums(4, to_message(p_sum, q_sum), send_final, send_final_rest)
    p_two, q_two = from_message(totals / count)

    def back_two(i):
        normed = (second[i] - mean_two) * inv_two
        scaled = outer[i] * gain_two
        return valid_row(i) * inv_two * (scaled - p_two - normed * q_two)

    keep_rows(GRAD_TWO, back_two)
    halo_start(GRAD_TWO)
    mirror_block(0)
    grad_taps(1, ACTIVE, d_two, GRAD_TWO)
    halo_wait(GRAD_TWO)
    mirror_block(1)
    spread(GRAD_TWO, d_two)
    gain_one = gain_b[0]

    def descend(i, out, carry):
        p_sum, q_sum = carry
        up_i = out * slope_one[i]
        inner[i] = up_i
        scaled = up_i * gain_one
        return p_sum + scaled, q_sum + scaled * ((first[i] - mean_one) * inv_one)

    p_sum, q_sum = convolve(GRAD_TWO, d_two, 3, descend, (nothing, nothing))

    def beside_inner():
        mirror_block(2)
        grad_taps_across(1)

    totals = sums(6, to_message(p_sum, q_sum), beside_inner, lambda: mirror_block(3))
    p_one, q_one = from_message(totals / count)

    def back_one(i):
        normed = (first[i] - mean_one) * inv_one
        scaled = inner[i] * gain_one
        return valid_row(i) * inv_one * (scaled - p_one - normed * q_one)

    keep_rows(GRAD_ONE, back_one)
    halo_start(GRAD_ONE)
    grad_taps(0, PAIRS, d_one, GRAD_ONE)
    grad_taps_back(1)
    halo_wait(GRAD_ONE)
    spread(GRAD_ONE, d_one)

    def lower(i, out, carry):
        S[pl.ds(i, CH, stride=RT), :] = (outer[i] + out) * valid_row(i)
        return carry

    convolve(GRAD_ONE, d_one, 1, lower, 0)

    def keep_grad(g, _):
        block = S[pl.ds(pl.multiple_of(128 * g, 128), 128), :]
        gp_out[pl.ds(4 * g, 4)] = block.reshape(4, RT, CT).astype(BF16)
        return 0

    lax.fori_loop(0, 16, keep_grad, 0)
    move_tile(4, gp_out.at[lower_half], gp_ref.at[lower_half], keeper)
    grad_taps_across(0)
    moved(2, fin_in.at[lower_half])
    moved(3, fin_in.at[upper_half])
    mirror_wait(1)

    def join_final(g, _):
        def use(c, flip):
            sym_ref[c] = ((fin_in[c].astype(F32) + flip) * 0.5).astype(BF16)

        mirror_step(1, g, use)
        return 0

    lax.fori_loop(0, 16, join_final, 0)
    grad_taps_back(0)
    move_tile(5, gp_out.at[upper_half], gp_ref.at[upper_half], keeper)
    grad_taps_end(1)
    grad_taps_end(0)

    sent_tile(0, pin, worker)
    sent_tile(1, cin, worker)
    for k in (2, 3, 4, 5):
        sent_tile(k, fin_out.at[lower_half], keeper)
    cross_sent()
    mirror_sent()
    for q in range(8):
        size = G2 if q % 2 else G1
        wait_bytes(ar_r.at[q, pl.ds(0, size - 1)], ar_send_sem.at[q])
    for k in range(2):
        wait_bytes(w_a.at[k, pl.ds(0, G1 - 1)], w_send_sem.at[k, 0])
        wait_bytes(w_b.at[k, pl.ds(0, G2 - 1)], w_send_sem.at[k, 1])
        wait_bytes(w_c.at[k, pl.ds(0, G1 - 1)], w_send_sem.at[k, 2])
    moved(4, gp_out.at[lower_half])
    moved(5, gp_out.at[upper_half])


def solution(mesh):
    R, C = mesh.shape["row"], mesh.shape["col"]

    def per_device(pairs, w_first, w_second, gains, shifts, dilations, residue_count, cotangent):
        CH, RT, CT = pairs.shape
        G1, G2 = 2 * C, R // 2
        G, share = max(G1, G2), 16 // G1
        vmem = pl.BlockSpec(memory_space=pltpu.VMEM)
        smem = pl.BlockSpec(memory_space=pltpu.SMEM)
        anywhere = pl.BlockSpec(memory_space=pl.ANY)
        tile = pltpu.VMEM((CH, RT, CT), BF16)
        field = pltpu.VMEM((RT, CH, CT), F32)
        flat = pltpu.VMEM((CH * RT, CT), F32)
        dma = pltpu.SemaphoreType.DMA
        return pl.pallas_call(
            functools.partial(kernel, R, C),
            out_shape=(
                jax.ShapeDtypeStruct((CH, RT, CT), BF16),
                jax.ShapeDtypeStruct((CH, RT, CT), BF16),
                jax.ShapeDtypeStruct((2, 3, 3, CH, CH), F32),
            ),
            in_specs=[smem, smem, anywhere, vmem, vmem, vmem, vmem, vmem],
            out_specs=(vmem, anywhere, vmem),
            scratch_shapes=[
                tile,
                tile,
                tile,
                tile,
                tile,
                pltpu.VMEM((2, 4, 16, RT, CT), BF16),
                pltpu.VMEM((2, 4, 16, RT, CT), BF16),
                pltpu.VMEM((G2, 16, RT, CT), BF16),
                pltpu.VMEM((4, RT + 2 * EDGE, CH, CT), BF16),
                pltpu.VMEM((4, 2, 4, CH, CT), BF16),
                pltpu.VMEM((4, 2, 8, CH, CT), BF16),
                pltpu.VMEM((4, RT + 2 * EDGE, 3 * CH, CT), BF16),
                flat,
                flat,
                field,
                field,
                field,
                field,
                field,
                pltpu.VMEM((4, CH, 9 * CH), BF16),
                pltpu.VMEM((2, CH, CT), F32),
                pltpu.VMEM((2, CH, CT), F32),
                pltpu.VMEM((8, 1, CT), F32),
                pltpu.VMEM((8, G, 1, CT), F32),
                pltpu.VMEM((CH, 768), F32),
                pltpu.VMEM((2, G1, share, 8, 384), F32),
                pltpu.VMEM((2, G1, share, 8, 384), F32),
                pltpu.VMEM((2, share, 8, 384), F32),
                pltpu.VMEM((2, G2, share, 8, 384), F32),
                pltpu.VMEM((2, share, 8, 384), F32),
                pltpu.VMEM((2, G1, share, 8, 384), F32),
                dma((6,)),
                dma((6,)),
                dma((4, 8)),
                dma((4, 8)),
                dma((2, 4)),
                dma((2, 4)),
                dma((8,)),
                dma((8,)),
                dma((G2,)),
                dma((G2,)),
                dma((2, 3)),
                dma((2, 3)),
            ],
            compiler_params=pltpu.CompilerParams(
                collective_id=0, has_side_effects=True, vmem_limit_bytes=56 * 1024 * 1024
            ),
            cost_estimate=pl.CostEstimate(
                flops=6 * 2 * 9 * CH * CH * RT * CT, bytes_accessed=4 * CH * RT * CT, transcendentals=0
            ),
        )(dilations, residue_count, pairs, cotangent, w_first, w_second, gains, shifts)

    in_specs = (P(None, "row", "col"), P(), P(), P(), P(), P(), P(), P(None, "row", "col"))
    out_specs = (P(None, "row", "col"), P(None, "row", "col"), P())
    return jax.shard_map(
        per_device, mesh=mesh, in_specs=in_specs, out_specs=out_specs, check_vma=False
    )
```

```python
import functools

import jax
import jax.numpy as jnp
from jax import lax
from jax.experimental import pallas as pl
from jax.experimental.pallas import tpu as pltpu
from jax.sharding import PartitionSpec as P

MESH = pl.DeviceIdType.MESH
F32 = jnp.float32
BF16 = jnp.bfloat16
EPSILON = 1e-05
EDGE = 16
PAIRS, ACTIVE, GRAD_TWO, GRAD_ONE = range(4)
FIRST, SECOND, OUTER, INNER = range(4)
CHIPS = (2, 7, 6, 4, 3, 1, 0, 5)


def roll(x, shift):
    return pltpu.roll(x, shift, 1)


def kernel(
    R,
    C,
    dil_ref,
    count_ref,
    pairs_ref,
    cot_ref,
    w_first_ref,
    w_second_ref,
    gains_ref,
    shifts_ref,
    sym_ref,
    gp_ref,
    gw_ref,
    pin,
    cin,
    fin_out,
    fin_in,
    gp_out,
    mir_s,
    mir_r,
    relayed,
    ext,
    lat_s,
    lat_r,
    taps,
    S,
    Sb,
    wide,
    beside_s,
    beside_r,
    slope_one,
    wmat,
    gain_b,
    shift_b,
    ar_s,
    ar_r,
    w_acc,
    w_parts,
    w_a,
    w_b_s,
    w_b,
    w_c_s,
    w_c,
    tile_send,
    tile_recv,
    halo_send,
    halo_recv,
    mir_send,
    mir_recv,
    ar_send_sem,
    ar_recv_sem,
    relay_send,
    relay_recv,
    w_send_sem,
    w_recv_sem,
):
    CH, RT, CT = 64, 32, 128
    row = lax.axis_index("row")
    col = lax.axis_index("col")
    half = C // 2
    G1, G2 = 2 * C, R // 2
    share = 16 // G2
    m, p = row // 2, (row % 2) * C + col

    chips = CHIPS if C == len(CHIPS) else tuple(range(C))

    def pick(table, k):
        found = jnp.int32(0)
        for j, entry in enumerate(table):
            found = found + jnp.where(k == j, entry, 0)
        return found

    def place(tr, tc):
        z = pick(chips, tc)
        return 2 * (tr // 2) + z // half, 2 * (z % half) + tr % 2

    def tile_of(r, c):
        z = (r % 2) * half + c // 2
        return 2 * (r // 2) + c % 2, pick([chips.index(j) for j in range(C)], z)

    def holder(tr, tc):
        return tr, tc

    lr, lc = tile_of(row, col)
    up, down = (lr + R - 1) % R, (lr + 1) % R
    left, right = (lc + C - 1) % C, (lc + 1) % C

    def is_me(target):
        return jnp.logical_and(target[0] == row, target[1] == col)

    def remote(src, dst, send, recv, target):
        return pltpu.make_async_remote_copy(
            src_ref=src,
            dst_ref=dst,
            send_sem=send,
            recv_sem=recv,
            device_id=target,
            device_id_type=MESH,
        )

    def wait_bytes(ref, sem):
        pltpu.make_async_copy(ref, ref, sem).wait()

    barrier = pltpu.get_barrier_semaphore()

    def greet(target):
        pl.semaphore_signal(barrier, inc=1, device_id=target, device_id_type=MESH)

    def greet_one(k, _):
        t = (p + k) % G1
        greet((2 * m + t // C, t % C))
        return 0

    def greet_two(k, _):
        t = (m + k) % G2
        greet((2 * t + row % 2, col))
        return 0

    lax.fori_loop(1, G1, greet_one, 0)
    lax.fori_loop(1, G2, greet_two, 0)
    across = (lr + R - 1 + 2 * (lr % 2)) % R
    for tc in (left, lc, right):
        greet(place(across, tc))
    expected = G1 - 1 + G2 - 1 + 3
    relays = m // 4 == col // 2

    def relay_of(b):
        mt = 2 * col + b // 2
        return 2 * mt + row % 2, 2 * (col // 2) + b % 2

    for b in range(4):
        expected = expected + jnp.logical_not(is_me(relay_of(b))).astype(jnp.int32)

    def greet_source(j, _):
        source = (2 * j + row % 2, m // 2)

        @pl.when(jnp.logical_and(relays, jnp.logical_not(is_me(source))))
        def _():
            greet(source)

        return 0

    lax.fori_loop(0, G2, greet_source, 0)

    n = count_ref[0]
    count = jnp.full((1, CT), 1.0, F32) * (n.astype(F32) * n.astype(F32))
    lane = lax.broadcasted_iota(jnp.int32, (CH, CT), 1)
    lane_row = lax.broadcasted_iota(jnp.int32, (1, CT), 1)
    col_valid = (lane + lc * CT < n).astype(F32)
    lane_block = lane // 16

    def valid_row(i):
        return jnp.where(lr * RT + i < n, col_valid, 0.0)

    def valid_wide(e):
        at = lr * RT + e - EDGE
        return jnp.where(jnp.logical_and(at >= 0, at < n), col_valid, 0.0)

    def valid_beside(side, g):
        at_row = lr * RT + 8 * g - EDGE + lane_block
        at_col = lc * CT + (CT if side else -EDGE) + lane % 16
        inside = jnp.logical_and(at_row >= 0, at_row < n)
        return jnp.where(jnp.logical_and(inside, jnp.logical_and(at_col >= 0, at_col < n)), 1.0, 0.0)

    for k, ref in enumerate((w_first_ref, w_second_ref)):
        blocks = [ref[a, b] for a in range(3) for b in range(3)]
        wmat[2 * k] = jnp.concatenate(blocks, axis=1)
        flipped = [blocks[8 - t].astype(F32).T.astype(BF16) for t in range(9)]
        wmat[2 * k + 1] = jnp.concatenate(flipped, axis=1)
    for k in range(2):
        gain_b[k] = jnp.broadcast_to(gains_ref[k : k + 1, :], (CT, CH)).T
        shift_b[k] = jnp.broadcast_to(shifts_ref[k : k + 1, :], (CT, CH)).T

    def move_tile(k, src, dst, target):
        either(src, dst, tile_send.at[k], tile_recv.at[k], target)

    def moved(k, dst):
        wait_bytes(dst, tile_recv.at[k])

    def sent_tile(k, src, target):
        @pl.when(jnp.logical_not(is_me(target)))
        def _():
            wait_bytes(src, tile_send.at[k])

    worker, keeper = place(row, col), holder(lr, lc)
    lower_half, upper_half = pl.ds(0, CH // 2), pl.ds(CH // 2, CH // 2)

    def mirror_pack(k, src):
        def step(g, _):
            turned = src[pl.ds(pl.multiple_of(128 * g, 128), 128), :].T
            for b in range(4):
                mir_s[k, b, g] = turned[32 * b : 32 * b + 32].astype(BF16)
            return 0

        lax.fori_loop(0, 16, step, 0)

    def either(src, dst, send, recv, target):
        @pl.when(is_me(target))
        def _():
            pltpu.make_async_copy(src, dst, recv).start()

        @pl.when(jnp.logical_not(is_me(target)))
        def _():
            remote(src, dst, send, recv, target).start()

    def cross_start():
        for b in range(4):
            either(mir_s.at[0, b], relayed.at[m], mir_send.at[0, b], relay_recv.at[m], relay_of(b))

    def cross_target(j):
        return place(2 * m + col % 2, j // 2)

    def cross_on(first, last):
        def step(j, _):
            @pl.when(relays)
            def _():
                wait_bytes(relayed.at[j], relay_recv.at[j])
                slot = 2 * (j % 2) + row % 2
                either(
                    relayed.at[j], mir_r.at[0, slot], relay_send.at[j], mir_recv.at[0, slot], cross_target(j)
                )

            return 0

        lax.fori_loop(first, last, step, 0)

    def cross_sent():
        for b in range(4):

            @pl.when(jnp.logical_not(is_me(relay_of(b))))
            def _(b=b):
                wait_bytes(mir_s.at[0, b], mir_send.at[0, b])

        def step(j, _):
            @pl.when(jnp.logical_and(relays, jnp.logical_not(is_me(cross_target(j)))))
            def _():
                wait_bytes(relayed.at[j], relay_send.at[j])

            return 0

        lax.fori_loop(0, G2, step, 0)

    def mirror_half(b, h):
        part, slot = pl.ds(8 * h, 8), lr % 4
        either(
            mir_s.at[1, b, part], mir_r.at[1, slot, part],
            mir_send.at[1, 2 * b + h], mir_recv.at[1, 2 * slot + h],
            holder(4 * lc + b, lr // 4),
        )

    def mirror_sent():
        for b in range(4):

            @pl.when(jnp.logical_not(is_me(holder(4 * lc + b, lr // 4))))
            def _(b=b):
                for h in range(2):
                    wait_bytes(mir_s.at[1, b, pl.ds(8 * h, 8)], mir_send.at[1, 2 * b + h])

    def mirror_wait(k):
        for s in range(4):
            if k == 0:
                wait_bytes(mir_r.at[k, s], mir_recv.at[k, s])
            else:
                for h in range(2):
                    wait_bytes(mir_r.at[k, s, pl.ds(8 * h, 8)], mir_recv.at[k, 2 * s + h])

    quarter = lax.broadcasted_iota(jnp.int32, (RT, CT), 1) // 32

    def mirror_step(k, g, use):
        got = [mir_r[k, s, g].astype(F32) for s in range(4)]
        for kk in range(4):
            flip = got[kk]
            for s in range(4):
                if s != kk:
                    flip = jnp.where(quarter == s, roll(got[s], (32 * (s - kk)) % 128), flip)
            use(4 * g + kk, flip)

    def to_channels(src, dst):
        def step(g, _):
            block = src[pl.ds(4 * g, 4)].astype(F32).reshape(128, 128)
            dst[pl.ds(pl.multiple_of(128 * g, 128), 128), :] = block
            return 0

        lax.fori_loop(0, 16, step, 0)

    to_channels(cot_ref, S)
    mirror_pack(0, S)
    pl.semaphore_wait(barrier, expected)
    move_tile(0, pairs_ref, pin, worker)
    cross_start()

    def pack_columns(value, put):
        def step(g, _):
            low = jnp.zeros((CH, CT), F32)
            high = jnp.zeros((CH, CT), F32)
            for q in range(8):
                v = value(8 * g + q)
                here = lane_block == q
                low = jnp.where(here, roll(v, 16 * q) if q else v, low)
                high = jnp.where(here, roll(v, (16 * q + 16) % 128) if q < 7 else v, high)
            put(g, low, high)
            return 0

        lax.fori_loop(0, 4, step, 0)

    def pairs_copies():
        own, low, high, got = ext, lat_s.at[0], lat_s.at[1], lat_r
        whole, top, bottom = pl.ds(0, 4), pl.ds(0, 2), pl.ds(2, 2)
        mid, head, tail = pl.ds(2, 4), pl.ds(0, 2), pl.ds(6, 2)
        plan = (
            (own.at[pl.ds(16, 16)], own.at[pl.ds(48, 16)], (up, lc)),
            (own.at[pl.ds(32, 16)], own.at[pl.ds(0, 16)], (down, lc)),
            (low.at[whole], got.at[1, mid], (lr, left)),
            (high.at[whole], got.at[0, mid], (lr, right)),
            (low.at[top], got.at[1, tail], (up, left)),
            (high.at[top], got.at[0, tail], (up, right)),
            (low.at[bottom], got.at[1, head], (down, left)),
            (high.at[bottom], got.at[0, head], (down, right)),
        )
        return [
            remote(src, dst, halo_send.at[0, k], halo_recv.at[0, k], place(*tile))
            for k, (src, dst, tile) in enumerate(plan)
        ]

    def field_copies(f):
        own, got = wide.at[f], beside_r.at[f]
        plan = (
            (own.at[pl.ds(16, 16)], own.at[pl.ds(48, 16)], (up, lc)),
            (own.at[pl.ds(32, 16)], own.at[pl.ds(0, 16)], (down, lc)),
            (beside_s.at[f, 0], got.at[1, pl.ds(2, 4)], (lr, left)),
            (beside_s.at[f, 1], got.at[0, pl.ds(2, 4)], (lr, right)),
            (got.at[0, pl.ds(2, 2)], got.at[0, pl.ds(6, 2)], (up, lc)),
            (got.at[1, pl.ds(2, 2)], got.at[1, pl.ds(6, 2)], (up, lc)),
            (got.at[0, pl.ds(4, 2)], got.at[0, pl.ds(0, 2)], (down, lc)),
            (got.at[1, pl.ds(4, 2)], got.at[1, pl.ds(0, 2)], (down, lc)),
        )
        return [
            remote(src, dst, halo_send.at[1 + f, k], halo_recv.at[1 + f, k], place(*tile))
            for k, (src, dst, tile) in enumerate(plan)
        ]

    def rows_start(f):
        for copy in field_copies(f)[:2]:
            copy.start()

    def columns_start(f):
        def put(g, low, high):
            beside_s[f, 0, g] = low
            beside_s[f, 1, g] = high

        pack_columns(lambda i: wide[f, EDGE + i], put)
        for copy in field_copies(f)[2:4]:
            copy.start()

    def corners_start(f):
        copies = field_copies(f)
        for copy in copies[2:4]:
            copy.wait()
        for copy in copies[4:]:
            copy.start()

    def field_wait(f):
        copies = field_copies(f)
        for copy in copies[:2] + copies[4:]:
            copy.wait()

    def pairs_start():
        def value(i):
            v = S[pl.ds(i, CH, stride=RT), :] * valid_row(i)
            ext[EDGE + i] = v.astype(BF16)
            return v

        def put(g, low, high):
            lat_s[0, g] = low.astype(BF16)
            lat_s[1, g] = high.astype(BF16)

        pack_columns(value, put)
        for copy in pairs_copies():
            copy.start()

    def pairs_wait():
        for copy in pairs_copies():
            copy.wait()
        rows16 = jnp.zeros((EDGE, CH, CT), BF16)
        two = jnp.zeros((2, CH, CT), BF16)
        eight = jnp.zeros((8, CH, CT), BF16)

        @pl.when(lr == 0)
        def _():
            ext[0:EDGE] = rows16
            lat_r[0, 0:2] = two
            lat_r[1, 0:2] = two

        @pl.when(lr == R - 1)
        def _():
            ext[EDGE + RT :] = rows16
            lat_r[0, 6:8] = two
            lat_r[1, 6:8] = two

        @pl.when(lc == 0)
        def _():
            lat_r[0] = eight

        @pl.when(lc == C - 1)
        def _():
            lat_r[1] = eight

    def spread(ph, d, value, beside):
        back_by, ahead_by = lane >= d, lane < CT - d

        def step(g, _):
            before, after = beside(0, g), beside(1, g)
            for q in range(8):
                e = 8 * g + q
                v = value(e)
                low = jnp.where(back_by, roll(v, d), roll(before, (240 + d - 16 * q) % CT))
                high = jnp.where(ahead_by, roll(v, CT - d), roll(after, (256 - d - 16 * q) % CT))
                taps[ph, e, 0:CH] = low.astype(BF16)
                taps[ph, e, CH : 2 * CH] = v.astype(BF16)
                taps[ph, e, 2 * CH :] = high.astype(BF16)
            return 0

        lax.fori_loop(0, 8, step, 0)

    def own_row(ph, i):
        return taps[ph, EDGE + i, CH : 2 * CH]

    def window(ph, d, i):
        rows = []
        for a in range(3):
            at = i + EDGE + (a - 1) * d
            rows.append(jnp.concatenate([taps[ph, at], taps[ph, at + 1]], axis=1))
        return jnp.concatenate(rows, axis=0)

    def convolve(ph, d, k, use, carry):
        weights = wmat[k]

        def step(t, carry):
            i = 2 * t
            out = jnp.dot(weights, window(ph, d, i), preferred_element_type=F32)
            carry = use(i, out[:, :CT], carry)
            return use(i + 1, out[:, CT:], carry)

        return lax.fori_loop(0, RT // 2, step, carry, unroll=4)

    def to_message(one, two):
        return jnp.sum(jnp.concatenate([one, two], axis=0).T, axis=0, keepdims=True)

    def from_message(msg):
        wide = jnp.broadcast_to(msg, (CT, CT)).T
        return wide[:CH], wide[CH:]

    def sum_start(q, msg):
        mine = m if q % 2 else p
        size = G2 if q % 2 else G1
        ar_s[q] = msg
        ar_r[q, mine] = msg

        def step(k, _):
            t = (mine + k) % size
            target = (2 * t + row % 2, col) if q % 2 else (2 * m + t // C, t % C)
            remote(ar_s.at[q], ar_r.at[q, mine], ar_send_sem.at[q], ar_recv_sem.at[q], target).start()
            return 0

        lax.fori_loop(1, size, step, 0)

    def sum_wait(q):
        size = G2 if q % 2 else G1
        wait_bytes(ar_r.at[q, pl.ds(0, size - 1)], ar_recv_sem.at[q])
        return [ar_r[q, t] for t in range(size)]

    def plain(parts):
        total = parts[0]
        for part in parts[1:]:
            total = total + part
        return total

    def wide_count(number):
        return jnp.full((1, CT), 1.0, F32) * number.astype(F32)

    def pooled(parts, numbers):
        counts = [wide_count(number) for number in numbers]
        total = plain(parts)
        mean = total / jnp.maximum(plain(counts), 1.0)
        apart = jnp.zeros((1, CT), F32)
        for part, number in zip(parts, counts):
            off = part / jnp.maximum(number, 1.0) - mean
            apart = apart + number * off * off
        return jnp.where(lane_row < CH, total, total + roll(apart, CH))

    def extent(start, size):
        return jnp.clip(n - start, 0, size)

    def tile_count(tr, tc):
        return extent(tr * RT, RT) * extent(tc * CT, CT)

    def sums(q, message, beside_one, beside_two):
        sum_start(q, message)
        beside_one()
        sum_start(q + 1, plain(sum_wait(q)))
        beside_two()
        return plain(sum_wait(q + 1))

    def norm(q, field, total, beside_one, beside_two):
        own = wide_count(tile_count(lr, lc))
        center = jnp.sum(total, axis=1, keepdims=True) / jnp.maximum(own, 1.0)

        def step(i, acc):
            off = (wide[field, EDGE + i] - center) * valid_row(i)
            return acc + off * off

        spread_sum = lax.fori_loop(0, RT, step, jnp.zeros((CH, CT), F32), unroll=4)
        sum_start(q, to_message(total, spread_sum))
        beside_one()
        parts = sum_wait(q)
        numbers = [tile_count(*tile_of(2 * m + t // C, t % C)) for t in range(G1)]
        sum_start(q + 1, pooled(parts, numbers))
        beside_two()
        parts = sum_wait(q + 1)
        numbers = [extent(2 * RT * t, 2 * RT) * n for t in range(G2)]
        mean, var = from_message(pooled(parts, numbers) / count)
        return mean, lax.rsqrt(var + EPSILON)

    def grad_taps(k, ph, d, grads):
        w_acc[...] = jnp.zeros(w_acc.shape, F32)

        def step(t, _):
            i = 4 * t
            g = jnp.concatenate([own_row(grads, i + j) for j in range(4)], axis=1)
            around = jnp.concatenate([window(ph, d, i), window(ph, d, i + 2)], axis=1)
            w_acc[:, : 9 * CH] += lax.dot_general(
                g, around, (((1,), (1,)), ((), ())), preferred_element_type=F32
            )
            return 0

        lax.fori_loop(0, RT // 4, step, 0, unroll=2)
        for t in range(16):
            r, c = 8 * (t // 2), 384 * (t % 2)
            w_parts[k, t // share, t % share] = w_acc[r : r + 8, c : c + 384]
        w_a[k, m] = w_parts[k, m]

        def send(j, _):
            t = (m + j) % G2
            remote(
                w_parts.at[k, t], w_a.at[k, m], w_send_sem.at[k, 0], w_recv_sem.at[k, 0],
                (2 * t + row % 2, col),
            ).start()
            return 0

        lax.fori_loop(1, G2, send, 0)

    def grad_taps_across(k):
        wait_bytes(w_a.at[k, pl.ds(0, G2 - 1)], w_recv_sem.at[k, 0])
        total = plain([w_a[k, t] for t in range(G2)])
        w_b_s[k] = total
        w_b[k, p] = total

        def send(j, _):
            t = (p + j) % G1
            remote(
                w_b_s.at[k], w_b.at[k, p], w_send_sem.at[k, 1], w_recv_sem.at[k, 1],
                (2 * m + t // C, t % C),
            ).start()
            return 0

        lax.fori_loop(1, G1, send, 0)

    def grad_taps_back(k):
        wait_bytes(w_b.at[k, pl.ds(0, G1 - 1)], w_recv_sem.at[k, 1])
        total = plain([w_b[k, t] for t in range(G1)])
        w_c_s[k] = total
        w_c[k, m] = total

        def send(j, _):
            t = (m + j) % G2
            remote(
                w_c_s.at[k], w_c.at[k, m], w_send_sem.at[k, 2], w_recv_sem.at[k, 2],
                (2 * t + row % 2, col),
            ).start()
            return 0

        lax.fori_loop(1, G2, send, 0)

    def grad_taps_end(k):
        wait_bytes(w_c.at[k, pl.ds(0, G2 - 1)], w_recv_sem.at[k, 2])
        for t in range(16):
            r, c = 8 * (t // 2), 384 * (t % 2)
            part = w_c[k, t // share, t % share]
            for tap in range(9):
                at = CH * tap - c
                if 0 <= at < 384:
                    gw_ref[k, tap // 3, tap % 3, r : r + 8, :] = part[:, at : at + CH]

    d_one, d_two = dil_ref[0], dil_ref[1]
    moved(0, pin)
    to_channels(pin, S)
    pairs_start()
    move_tile(1, cot_ref, cin, worker)
    pairs_wait()
    spread(
        PAIRS, d_one, lambda e: ext[e].astype(F32), lambda side, g: lat_r[side, g].astype(F32)
    )


    def keep(f):
        def use(i, out, total):
            wide[f, EDGE + i] = out
            return total + out * valid_row(i)

        return use

    nothing = jnp.zeros((CH, CT), F32)
    total = convolve(PAIRS, d_one, 0, keep(FIRST), nothing)
    rows_start(FIRST)

    def beside_first():
        columns_start(FIRST)
        cross_on(0 * G2 // 16, 10 * G2 // 16)

    mean_one, inv_one = norm(0, FIRST, total, beside_first, lambda: corners_start(FIRST))
    scale_one = inv_one * gain_b[0]
    shift_one = shift_b[0]

    def activate(raw, valid):
        level = (raw - mean_one) * scale_one + shift_one
        low = jnp.exp(jnp.minimum(level, 0.0))
        return jnp.where(level > 0.0, level, low - 1.0) * valid, low * valid

    def active_row(e):
        active, slope = activate(wide[FIRST, e], valid_wide(e))
        slope_one[e] = slope
        return active

    def active_beside(side, g):
        return activate(beside_r[FIRST, side, g], valid_beside(side, g))[0]

    field_wait(FIRST)
    spread(ACTIVE, d_two, active_row, active_beside)
    cross_on(10 * G2 // 16, 16 * G2 // 16)
    total = convolve(ACTIVE, d_two, 2, keep(SECOND), nothing)
    rows_start(SECOND)

    def join_cotangent():
        corners_start(SECOND)
        moved(1, cin)
        mirror_wait(0)

        def join(g, _):
            def use(c, flip):
                back = (cin[c].astype(F32) + flip) * 0.5
                Sb[pl.ds(pl.multiple_of(RT * c, RT), RT), :] = back

            mirror_step(0, g, use)
            return 0

        lax.fori_loop(0, 16, join, 0)

    mean_two, inv_two = norm(2, SECOND, total, lambda: columns_start(SECOND), join_cotangent)
    gain_two = gain_b[1]
    scale_two = inv_two * gain_two
    shift_two = shift_b[1]

    def finish(i, carry):
        p_sum, q_sum = carry
        off = wide[SECOND, EDGE + i] - mean_two
        before = own_row(PAIRS, i).astype(F32) + (off * scale_two + shift_two)
        low = jnp.exp(jnp.minimum(before, 0.0))
        valid = valid_row(i)
        S[pl.ds(i, CH, stride=RT), :] = jnp.where(before > 0.0, before, low - 1.0) * valid
        out = Sb[pl.ds(i, CH, stride=RT), :] * valid * low
        wide[OUTER, EDGE + i] = out
        scaled = out * gain_two
        return p_sum + scaled, q_sum + scaled * (off * inv_two)

    p_sum, q_sum = lax.fori_loop(0, RT, finish, (nothing, nothing), unroll=4)
    rows_start(OUTER)

    def send_final():
        columns_start(OUTER)

        def keep_final(g, _):
            block = S[pl.ds(pl.multiple_of(128 * g, 128), 128), :]
            fin_out[pl.ds(4 * g, 4)] = block.reshape(4, RT, CT).astype(BF16)
            return 0

        lax.fori_loop(0, 16, keep_final, 0)
        move_tile(2, fin_out.at[lower_half], fin_in.at[lower_half], keeper)
        move_tile(3, fin_out.at[upper_half], fin_in.at[upper_half], keeper)
        mirror_pack(1, S)

    def after_final():
        corners_start(OUTER)
        mirror_half(0, 0)
        mirror_half(0, 1)
        mirror_half(1, 0)
        mirror_half(1, 1)
        field_wait(SECOND)

    totals = sums(4, to_message(p_sum, q_sum), send_final, after_final)
    p_two, q_two = from_message(totals / count)

    def grad_two(second, outer, valid):
        normed = (second - mean_two) * inv_two
        return valid * inv_two * (outer * gain_two - p_two - normed * q_two)

    field_wait(OUTER)
    spread(
        GRAD_TWO,
        d_two,
        lambda e: grad_two(wide[SECOND, e], wide[OUTER, e], valid_wide(e)),
        lambda side, g: grad_two(
            beside_r[SECOND, side, g], beside_r[OUTER, side, g], valid_beside(side, g)
        ),
    )
    gain_one = gain_b[0]

    def descend(i, out, carry):
        p_sum, q_sum = carry
        up_i = out * slope_one[EDGE + i]
        wide[INNER, EDGE + i] = up_i
        scaled = up_i * gain_one
        return p_sum + scaled, q_sum + scaled * ((wide[FIRST, EDGE + i] - mean_one) * inv_one)

    p_sum, q_sum = convolve(GRAD_TWO, d_two, 3, descend, (nothing, nothing))
    rows_start(INNER)

    def after_inner():
        corners_start(INNER)
        grad_taps_across(1)

    def beside_inner():
        columns_start(INNER)
        grad_taps(1, ACTIVE, d_two, GRAD_TWO)

    totals = sums(6, to_message(p_sum, q_sum), beside_inner, after_inner)
    p_one, q_one = from_message(totals / count)

    def grad_one(first, inner, valid):
        normed = (first - mean_one) * inv_one
        return valid * inv_one * (inner * gain_one - p_one - normed * q_one)

    field_wait(INNER)
    mirror_half(2, 0)
    mirror_half(2, 1)
    mirror_half(3, 0)
    mirror_half(3, 1)
    spread(
        GRAD_ONE,
        d_one,
        lambda e: grad_one(wide[FIRST, e], wide[INNER, e], valid_wide(e)),
        lambda side, g: grad_one(
            beside_r[FIRST, side, g], beside_r[INNER, side, g], valid_beside(side, g)
        ),
    )
    grad_taps(0, PAIRS, d_one, GRAD_ONE)
    grad_taps_back(1)

    def lower(i, out, carry):
        S[pl.ds(i, CH, stride=RT), :] = (wide[OUTER, EDGE + i] + out) * valid_row(i)
        return carry

    convolve(GRAD_ONE, d_one, 1, lower, 0)

    def keep_grad(g, _):
        block = S[pl.ds(pl.multiple_of(128 * g, 128), 128), :]
        gp_out[pl.ds(4 * g, 4)] = block.reshape(4, RT, CT).astype(BF16)
        return 0

    lax.fori_loop(0, 16, keep_grad, 0)
    grad_taps_across(0)
    move_tile(4, gp_out.at[lower_half], gp_ref.at[lower_half], keeper)
    move_tile(5, gp_out.at[upper_half], gp_ref.at[upper_half], keeper)
    moved(2, fin_in.at[lower_half])
    moved(3, fin_in.at[upper_half])
    mirror_wait(1)

    def join_final(g, _):
        def use(c, flip):
            sym_ref[c] = ((fin_in[c].astype(F32) + flip) * 0.5).astype(BF16)

        mirror_step(1, g, use)
        return 0

    lax.fori_loop(0, 16, join_final, 0)
    grad_taps_back(0)
    grad_taps_end(1)
    grad_taps_end(0)

    sent_tile(0, pin, worker)
    sent_tile(1, cin, worker)
    for k in (2, 3, 4, 5):
        sent_tile(k, fin_out.at[lower_half], keeper)
    cross_sent()
    mirror_sent()
    for q in range(8):
        size = G2 if q % 2 else G1
        wait_bytes(ar_r.at[q, pl.ds(0, size - 1)], ar_send_sem.at[q])
    for k in range(2):
        wait_bytes(w_a.at[k, pl.ds(0, G2 - 1)], w_send_sem.at[k, 0])
        wait_bytes(w_b.at[k, pl.ds(0, G1 - 1)], w_send_sem.at[k, 1])
        wait_bytes(w_c.at[k, pl.ds(0, G2 - 1)], w_send_sem.at[k, 2])
    moved(4, gp_out.at[lower_half])
    moved(5, gp_out.at[upper_half])


def solution(mesh):
    R, C = mesh.shape["row"], mesh.shape["col"]

    def per_device(pairs, w_first, w_second, gains, shifts, dilations, residue_count, cotangent):
        CH, RT, CT = pairs.shape
        G1, G2 = 2 * C, R // 2
        G, share = max(G1, G2), 16 // G2
        vmem = pl.BlockSpec(memory_space=pltpu.VMEM)
        smem = pl.BlockSpec(memory_space=pltpu.SMEM)
        anywhere = pl.BlockSpec(memory_space=pl.ANY)
        tile = pltpu.VMEM((CH, RT, CT), BF16)
        flat = pltpu.VMEM((CH * RT, CT), F32)
        dma = pltpu.SemaphoreType.DMA
        return pl.pallas_call(
            functools.partial(kernel, R, C),
            out_shape=(
                jax.ShapeDtypeStruct((CH, RT, CT), BF16),
                jax.ShapeDtypeStruct((CH, RT, CT), BF16),
                jax.ShapeDtypeStruct((2, 3, 3, CH, CH), F32),
            ),
            in_specs=[smem, smem, anywhere, vmem, vmem, vmem, vmem, vmem],
            out_specs=(vmem, anywhere, vmem),
            scratch_shapes=[
                tile,
                tile,
                tile,
                tile,
                tile,
                pltpu.VMEM((2, 4, 16, RT, CT), BF16),
                pltpu.VMEM((2, 4, 16, RT, CT), BF16),
                pltpu.VMEM((G2, 16, RT, CT), BF16),
                pltpu.VMEM((RT + 2 * EDGE, CH, CT), BF16),
                pltpu.VMEM((2, 4, CH, CT), BF16),
                pltpu.VMEM((2, 8, CH, CT), BF16),
                pltpu.VMEM((4, RT + 2 * EDGE, 3 * CH, CT), BF16),
                flat,
                flat,
                pltpu.VMEM((4, RT + 2 * EDGE, CH, CT), F32),
                pltpu.VMEM((4, 2, 4, CH, CT), F32),
                pltpu.VMEM((4, 2, 8, CH, CT), F32),
                pltpu.VMEM((RT + 2 * EDGE, CH, CT), F32),
                pltpu.VMEM((4, CH, 9 * CH), BF16),
                pltpu.VMEM((2, CH, CT), F32),
                pltpu.VMEM((2, CH, CT), F32),
                pltpu.VMEM((8, 1, CT), F32),
                pltpu.VMEM((8, G, 1, CT), F32),
                pltpu.VMEM((CH, 768), F32),
                pltpu.VMEM((2, G2, share, 8, 384), F32),
                pltpu.VMEM((2, G2, share, 8, 384), F32),
                pltpu.VMEM((2, share, 8, 384), F32),
                pltpu.VMEM((2, G1, share, 8, 384), F32),
                pltpu.VMEM((2, share, 8, 384), F32),
                pltpu.VMEM((2, G2, share, 8, 384), F32),
                dma((6,)),
                dma((6,)),
                dma((5, 8)),
                dma((5, 8)),
                dma((2, 8)),
                dma((2, 8)),
                dma((8,)),
                dma((8,)),
                dma((G2,)),
                dma((G2,)),
                dma((2, 3)),
                dma((2, 3)),
            ],
            compiler_params=pltpu.CompilerParams(
                collective_id=0, has_side_effects=True, vmem_limit_bytes=56 * 1024 * 1024
            ),
            cost_estimate=pl.CostEstimate(
                flops=6 * 2 * 9 * CH * CH * RT * CT, bytes_accessed=4 * CH * RT * CT, transcendentals=0
            ),
        )(dilations, residue_count, pairs, cotangent, w_first, w_second, gains, shifts)

    in_specs = (P(None, "row", "col"), P(), P(), P(), P(), P(), P(), P(None, "row", "col"))
    out_specs = (P(None, "row", "col"), P(None, "row", "col"), P())
    return jax.shard_map(
        per_device, mesh=mesh, in_specs=in_specs, out_specs=out_specs, check_vma=False
    )
```

```python
import functools

import jax
import jax.numpy as jnp
from jax import lax
from jax.experimental import pallas as pl
from jax.experimental.pallas import tpu as pltpu
from jax.sharding import PartitionSpec as P

MESH = pl.DeviceIdType.MESH
F32 = jnp.float32
BF16 = jnp.bfloat16
EPSILON = 1e-05
EDGE = 16
PAIRS, ACTIVE, GRAD_TWO, GRAD_ONE = range(4)
FIRST, SECOND, OUTER, INNER = range(4)
CHIPS = (2, 7, 6, 4, 3, 1, 0, 5)


def roll(x, shift):
    return pltpu.roll(x, shift, 1)


def kernel(
    R,
    C,
    dil_ref,
    count_ref,
    pairs_ref,
    cot_ref,
    w_first_ref,
    w_second_ref,
    gains_ref,
    shifts_ref,
    sym_ref,
    gp_ref,
    gw_ref,
    pin,
    cin,
    fin_out,
    fin_in,
    gp_out,
    mir_s,
    mir_r,
    relayed,
    ext,
    lat_s,
    lat_r,
    taps,
    S,
    Sb,
    wide,
    beside_s,
    beside_r,
    slope_one,
    wmat,
    gain_b,
    shift_b,
    ar_s,
    ar_r,
    w_acc,
    w_parts,
    w_a,
    w_b_s,
    w_b,
    w_c_s,
    w_c,
    tile_send,
    tile_recv,
    halo_send,
    halo_recv,
    mir_send,
    mir_recv,
    ar_send_sem,
    ar_recv_sem,
    relay_send,
    relay_recv,
    w_send_sem,
    w_recv_sem,
):
    CH, RT, CT = 64, 32, 128
    row = lax.axis_index("row")
    col = lax.axis_index("col")
    half = C // 2
    G1, G2 = 2 * C, R // 2
    share = 16 // G2
    m, p = row // 2, (row % 2) * C + col

    chips = CHIPS if C == len(CHIPS) else tuple(range(C))

    def pick(table, k):
        found = jnp.int32(0)
        for j, entry in enumerate(table):
            found = found + jnp.where(k == j, entry, 0)
        return found

    def place(tr, tc):
        z = pick(chips, tc)
        return 2 * (tr // 2) + z // half, 2 * (z % half) + tr % 2

    def tile_of(r, c):
        z = (r % 2) * half + c // 2
        return 2 * (r // 2) + c % 2, pick([chips.index(j) for j in range(C)], z)

    def holder(tr, tc):
        return tr, tc

    lr, lc = tile_of(row, col)
    up, down = (lr + R - 1) % R, (lr + 1) % R
    left, right = (lc + C - 1) % C, (lc + 1) % C

    def is_me(target):
        return jnp.logical_and(target[0] == row, target[1] == col)

    def remote(src, dst, send, recv, target):
        return pltpu.make_async_remote_copy(
            src_ref=src,
            dst_ref=dst,
            send_sem=send,
            recv_sem=recv,
            device_id=target,
            device_id_type=MESH,
        )

    def wait_bytes(ref, sem):
        pltpu.make_async_copy(ref, ref, sem).wait()

    barrier = pltpu.get_barrier_semaphore()

    def greet(target):
        pl.semaphore_signal(barrier, inc=1, device_id=target, device_id_type=MESH)

    def greet_one(k, _):
        t = (p + k) % G1
        greet((2 * m + t // C, t % C))
        return 0

    def greet_two(k, _):
        t = (m + k) % G2
        greet((2 * t + row % 2, col))
        return 0

    lax.fori_loop(1, G1, greet_one, 0)
    lax.fori_loop(1, G2, greet_two, 0)
    across = (lr + R - 1 + 2 * (lr % 2)) % R
    for tc in (left, lc, right):
        greet(place(across, tc))
    expected = G1 - 1 + G2 - 1 + 3
    relays = m // 4 == col // 2

    def relay_of(b):
        mt = 2 * col + b // 2
        return 2 * mt + row % 2, 2 * (col // 2) + b % 2

    for b in range(4):
        expected = expected + jnp.logical_not(is_me(relay_of(b))).astype(jnp.int32)

    def greet_source(j, _):
        source = (2 * j + row % 2, m // 2)

        @pl.when(jnp.logical_and(relays, jnp.logical_not(is_me(source))))
        def _():
            greet(source)

        return 0

    lax.fori_loop(0, G2, greet_source, 0)

    n = count_ref[0]
    count = jnp.full((1, CT), 1.0, F32) * (n.astype(F32) * n.astype(F32))
    lane = lax.broadcasted_iota(jnp.int32, (CH, CT), 1)
    lane_row = lax.broadcasted_iota(jnp.int32, (1, CT), 1)
    col_valid = (lane + lc * CT < n).astype(F32)
    lane_block = lane // 16

    def valid_row(i):
        return jnp.where(lr * RT + i < n, col_valid, 0.0)

    def valid_wide(e):
        at = lr * RT + e - EDGE
        return jnp.where(jnp.logical_and(at >= 0, at < n), col_valid, 0.0)

    def valid_beside(side, g):
        at_row = lr * RT + 8 * g - EDGE + lane_block
        at_col = lc * CT + (CT if side else -EDGE) + lane % 16
        inside = jnp.logical_and(at_row >= 0, at_row < n)
        return jnp.where(jnp.logical_and(inside, jnp.logical_and(at_col >= 0, at_col < n)), 1.0, 0.0)

    for k, ref in enumerate((w_first_ref, w_second_ref)):
        blocks = [ref[a, b] for a in range(3) for b in range(3)]
        wmat[2 * k] = jnp.concatenate(blocks, axis=1)
        flipped = [blocks[8 - t].astype(F32).T.astype(BF16) for t in range(9)]
        wmat[2 * k + 1] = jnp.concatenate(flipped, axis=1)
    for k in range(2):
        gain_b[k] = jnp.broadcast_to(gains_ref[k : k + 1, :], (CT, CH)).T
        shift_b[k] = jnp.broadcast_to(shifts_ref[k : k + 1, :], (CT, CH)).T

    def move_tile(k, src, dst, target):
        either(src, dst, tile_send.at[k], tile_recv.at[k], target)

    def moved(k, dst):
        wait_bytes(dst, tile_recv.at[k])

    def sent_tile(k, src, target):
        @pl.when(jnp.logical_not(is_me(target)))
        def _():
            wait_bytes(src, tile_send.at[k])

    worker, keeper = place(row, col), holder(lr, lc)
    lower_half, upper_half = pl.ds(0, CH // 2), pl.ds(CH // 2, CH // 2)

    def mirror_pack(k, src):
        def step(g, _):
            turned = src[pl.ds(pl.multiple_of(128 * g, 128), 128), :].T
            for b in range(4):
                mir_s[k, b, g] = turned[32 * b : 32 * b + 32].astype(BF16)
            return 0

        lax.fori_loop(0, 16, step, 0)

    def either(src, dst, send, recv, target):
        @pl.when(is_me(target))
        def _():
            pltpu.make_async_copy(src, dst, recv).start()

        @pl.when(jnp.logical_not(is_me(target)))
        def _():
            remote(src, dst, send, recv, target).start()

    def cross_start():
        for b in range(4):
            either(mir_s.at[0, b], relayed.at[m], mir_send.at[0, b], relay_recv.at[m], relay_of(b))

    def cross_target(j):
        return place(2 * m + col % 2, j // 2)

    def cross_on(first, last):
        def step(j, _):
            @pl.when(relays)
            def _():
                wait_bytes(relayed.at[j], relay_recv.at[j])
                slot = 2 * (j % 2) + row % 2
                either(
                    relayed.at[j], mir_r.at[0, slot], relay_send.at[j], mir_recv.at[0, slot], cross_target(j)
                )

            return 0

        lax.fori_loop(first, last, step, 0)

    def cross_sent():
        for b in range(4):

            @pl.when(jnp.logical_not(is_me(relay_of(b))))
            def _(b=b):
                wait_bytes(mir_s.at[0, b], mir_send.at[0, b])

        def step(j, _):
            @pl.when(jnp.logical_and(relays, jnp.logical_not(is_me(cross_target(j)))))
            def _():
                wait_bytes(relayed.at[j], relay_send.at[j])

            return 0

        lax.fori_loop(0, G2, step, 0)

    def mirror_half(b, h):
        part, slot = pl.ds(8 * h, 8), lr % 4
        either(
            mir_s.at[1, b, part], mir_r.at[1, slot, part],
            mir_send.at[1, 2 * b + h], mir_recv.at[1, 2 * slot + h],
            holder(4 * lc + b, lr // 4),
        )

    def mirror_sent():
        for b in range(4):

            @pl.when(jnp.logical_not(is_me(holder(4 * lc + b, lr // 4))))
            def _(b=b):
                for h in range(2):
                    wait_bytes(mir_s.at[1, b, pl.ds(8 * h, 8)], mir_send.at[1, 2 * b + h])

    def mirror_wait(k):
        for s in range(4):
            if k == 0:
                wait_bytes(mir_r.at[k, s], mir_recv.at[k, s])
            else:
                for h in range(2):
                    wait_bytes(mir_r.at[k, s, pl.ds(8 * h, 8)], mir_recv.at[k, 2 * s + h])

    quarter = lax.broadcasted_iota(jnp.int32, (RT, CT), 1) // 32

    def mirror_step(k, g, use):
        got = [mir_r[k, s, g].astype(F32) for s in range(4)]
        for kk in range(4):
            flip = got[kk]
            for s in range(4):
                if s != kk:
                    flip = jnp.where(quarter == s, roll(got[s], (32 * (s - kk)) % 128), flip)
            use(4 * g + kk, flip)

    def to_channels(src, dst):
        def step(g, _):
            block = src[pl.ds(4 * g, 4)].astype(F32).reshape(128, 128)
            dst[pl.ds(pl.multiple_of(128 * g, 128), 128), :] = block
            return 0

        lax.fori_loop(0, 16, step, 0)

    to_channels(cot_ref, S)
    mirror_pack(0, S)
    pl.semaphore_wait(barrier, expected)
    move_tile(0, pairs_ref, pin, worker)
    cross_start()

    def pack_columns(value, put):
        def step(g, _):
            low = jnp.zeros((CH, CT), F32)
            high = jnp.zeros((CH, CT), F32)
            for q in range(8):
                v = value(8 * g + q)
                here = lane_block == q
                low = jnp.where(here, roll(v, 16 * q) if q else v, low)
                high = jnp.where(here, roll(v, (16 * q + 16) % 128) if q < 7 else v, high)
            put(g, low, high)
            return 0

        lax.fori_loop(0, 4, step, 0)

    def pairs_copies():
        own, low, high, got = ext, lat_s.at[0], lat_s.at[1], lat_r
        whole, top, bottom = pl.ds(0, 4), pl.ds(0, 2), pl.ds(2, 2)
        mid, head, tail = pl.ds(2, 4), pl.ds(0, 2), pl.ds(6, 2)
        plan = (
            (own.at[pl.ds(16, 16)], own.at[pl.ds(48, 16)], (up, lc)),
            (own.at[pl.ds(32, 16)], own.at[pl.ds(0, 16)], (down, lc)),
            (low.at[whole], got.at[1, mid], (lr, left)),
            (high.at[whole], got.at[0, mid], (lr, right)),
            (low.at[top], got.at[1, tail], (up, left)),
            (high.at[top], got.at[0, tail], (up, right)),
            (low.at[bottom], got.at[1, head], (down, left)),
            (high.at[bottom], got.at[0, head], (down, right)),
        )
        return [
            remote(src, dst, halo_send.at[0, k], halo_recv.at[0, k], place(*tile))
            for k, (src, dst, tile) in enumerate(plan)
        ]

    def field_copies(f):
        own, got = wide.at[f], beside_r.at[f]
        plan = (
            (own.at[pl.ds(16, 16)], own.at[pl.ds(48, 16)], (up, lc)),
            (own.at[pl.ds(32, 16)], own.at[pl.ds(0, 16)], (down, lc)),
            (beside_s.at[f, 0], got.at[1, pl.ds(2, 4)], (lr, left)),
            (beside_s.at[f, 1], got.at[0, pl.ds(2, 4)], (lr, right)),
            (got.at[0, pl.ds(2, 2)], got.at[0, pl.ds(6, 2)], (up, lc)),
            (got.at[1, pl.ds(2, 2)], got.at[1, pl.ds(6, 2)], (up, lc)),
            (got.at[0, pl.ds(4, 2)], got.at[0, pl.ds(0, 2)], (down, lc)),
            (got.at[1, pl.ds(4, 2)], got.at[1, pl.ds(0, 2)], (down, lc)),
        )
        return [
            remote(src, dst, halo_send.at[1 + f, k], halo_recv.at[1 + f, k], place(*tile))
            for k, (src, dst, tile) in enumerate(plan)
        ]

    def rows_start(f):
        for copy in field_copies(f)[:2]:
            copy.start()

    def columns_start(f):
        def put(g, low, high):
            beside_s[f, 0, g] = low
            beside_s[f, 1, g] = high

        pack_columns(lambda i: wide[f, EDGE + i], put)
        for copy in field_copies(f)[2:4]:
            copy.start()

    def corners_start(f):
        copies = field_copies(f)
        for copy in copies[2:4]:
            copy.wait()
        for copy in copies[4:]:
            copy.start()

    def field_wait(f):
        copies = field_copies(f)
        for copy in copies[:2] + copies[4:]:
            copy.wait()

    def pairs_start():
        def value(i):
            v = S[pl.ds(i, CH, stride=RT), :] * valid_row(i)
            ext[EDGE + i] = v.astype(BF16)
            return v

        def put(g, low, high):
            lat_s[0, g] = low.astype(BF16)
            lat_s[1, g] = high.astype(BF16)

        pack_columns(value, put)
        for copy in pairs_copies():
            copy.start()

    def pairs_wait():
        for copy in pairs_copies():
            copy.wait()
        rows16 = jnp.zeros((EDGE, CH, CT), BF16)
        two = jnp.zeros((2, CH, CT), BF16)
        eight = jnp.zeros((8, CH, CT), BF16)

        @pl.when(lr == 0)
        def _():
            ext[0:EDGE] = rows16
            lat_r[0, 0:2] = two
            lat_r[1, 0:2] = two

        @pl.when(lr == R - 1)
        def _():
            ext[EDGE + RT :] = rows16
            lat_r[0, 6:8] = two
            lat_r[1, 6:8] = two

        @pl.when(lc == 0)
        def _():
            lat_r[0] = eight

        @pl.when(lc == C - 1)
        def _():
            lat_r[1] = eight

    def spread(ph, d, value, beside):
        back_by, ahead_by = lane >= d, lane < CT - d

        def step(g, _):
            before, after = beside(0, g), beside(1, g)
            for q in range(8):
                e = 8 * g + q
                v = value(e)
                low = jnp.where(back_by, roll(v, d), roll(before, (240 + d - 16 * q) % CT))
                high = jnp.where(ahead_by, roll(v, CT - d), roll(after, (256 - d - 16 * q) % CT))
                taps[ph, e, 0:CH] = low.astype(BF16)
                taps[ph, e, CH : 2 * CH] = v.astype(BF16)
                taps[ph, e, 2 * CH :] = high.astype(BF16)
            return 0

        lax.fori_loop(0, 8, step, 0)

    def own_row(ph, i):
        return taps[ph, EDGE + i, CH : 2 * CH]

    def window(ph, d, i):
        rows = []
        for a in range(3):
            at = i + EDGE + (a - 1) * d
            rows.append(jnp.concatenate([taps[ph, at], taps[ph, at + 1]], axis=1))
        return jnp.concatenate(rows, axis=0)

    def convolve(ph, d, k, use, carry):
        weights = wmat[k]

        def step(t, carry):
            i = 2 * t
            out = jnp.dot(weights, window(ph, d, i), preferred_element_type=F32)
            carry = use(i, out[:, :CT], carry)
            return use(i + 1, out[:, CT:], carry)

        return lax.fori_loop(0, RT // 2, step, carry, unroll=4)

    def to_message(one, two):
        return jnp.sum(jnp.concatenate([one, two], axis=0).T, axis=0, keepdims=True)

    def from_message(msg):
        wide = jnp.broadcast_to(msg, (CT, CT)).T
        return wide[:CH], wide[CH:]

    def sum_start(q, msg):
        mine = m if q % 2 else p
        size = G2 if q % 2 else G1
        ar_s[q] = msg
        ar_r[q, mine] = msg

        def step(k, _):
            t = (mine + k) % size
            target = (2 * t + row % 2, col) if q % 2 else (2 * m + t // C, t % C)
            remote(ar_s.at[q], ar_r.at[q, mine], ar_send_sem.at[q], ar_recv_sem.at[q], target).start()
            return 0

        lax.fori_loop(1, size, step, 0)

    def sum_wait(q):
        size = G2 if q % 2 else G1
        wait_bytes(ar_r.at[q, pl.ds(0, size - 1)], ar_recv_sem.at[q])
        return [ar_r[q, t] for t in range(size)]

    def plain(parts):
        total = parts[0]
        for part in parts[1:]:
            total = total + part
        return total

    def wide_count(number):
        return jnp.full((1, CT), 1.0, F32) * number.astype(F32)

    def pooled(parts, numbers):
        counts = [wide_count(number) for number in numbers]
        total = plain(parts)
        mean = total / jnp.maximum(plain(counts), 1.0)
        apart = jnp.zeros((1, CT), F32)
        for part, number in zip(parts, counts):
            off = part / jnp.maximum(number, 1.0) - mean
            apart = apart + number * off * off
        return jnp.where(lane_row < CH, total, total + roll(apart, CH))

    def extent(start, size):
        return jnp.clip(n - start, 0, size)

    def tile_count(tr, tc):
        return extent(tr * RT, RT) * extent(tc * CT, CT)

    def sums(q, message, beside_one, beside_two):
        sum_start(q, message)
        beside_one()
        sum_start(q + 1, plain(sum_wait(q)))
        beside_two()
        return plain(sum_wait(q + 1))

    def norm(q, field, total, beside_one, beside_two):
        own = wide_count(tile_count(lr, lc))
        center = jnp.sum(total, axis=1, keepdims=True) / jnp.maximum(own, 1.0)

        def step(i, acc):
            off = (wide[field, EDGE + i] - center) * valid_row(i)
            return acc + off * off

        spread_sum = lax.fori_loop(0, RT, step, jnp.zeros((CH, CT), F32), unroll=4)
        sum_start(q, to_message(total, spread_sum))
        beside_one()
        parts = sum_wait(q)
        numbers = [tile_count(*tile_of(2 * m + t // C, t % C)) for t in range(G1)]
        sum_start(q + 1, pooled(parts, numbers))
        beside_two()
        parts = sum_wait(q + 1)
        numbers = [extent(2 * RT * t, 2 * RT) * n for t in range(G2)]
        mean, var = from_message(pooled(parts, numbers) / count)
        return mean, lax.rsqrt(var + EPSILON)

    def grad_taps(k, ph, d, grads):
        w_acc[...] = jnp.zeros(w_acc.shape, F32)

        def step(t, _):
            i = 4 * t
            g = jnp.concatenate([own_row(grads, i + j) for j in range(4)], axis=1)
            around = jnp.concatenate([window(ph, d, i), window(ph, d, i + 2)], axis=1)
            w_acc[:, : 9 * CH] += lax.dot_general(
                g, around, (((1,), (1,)), ((), ())), preferred_element_type=F32
            )
            return 0

        lax.fori_loop(0, RT // 4, step, 0, unroll=2)
        for t in range(16):
            r, c = 8 * (t // 2), 384 * (t % 2)
            w_parts[k, t // share, t % share] = w_acc[r : r + 8, c : c + 384]
        w_a[k, m] = w_parts[k, m]

        def send(j, _):
            t = (m + j) % G2
            remote(
                w_parts.at[k, t], w_a.at[k, m], w_send_sem.at[k, 0], w_recv_sem.at[k, 0],
                (2 * t + row % 2, col),
            ).start()
            return 0

        lax.fori_loop(1, G2, send, 0)

    def grad_taps_across(k):
        wait_bytes(w_a.at[k, pl.ds(0, G2 - 1)], w_recv_sem.at[k, 0])
        total = plain([w_a[k, t] for t in range(G2)])
        w_b_s[k] = total
        w_b[k, p] = total

        def send(j, _):
            t = (p + j) % G1
            remote(
                w_b_s.at[k], w_b.at[k, p], w_send_sem.at[k, 1], w_recv_sem.at[k, 1],
                (2 * m + t // C, t % C),
            ).start()
            return 0

        lax.fori_loop(1, G1, send, 0)

    def grad_taps_back(k):
        wait_bytes(w_b.at[k, pl.ds(0, G1 - 1)], w_recv_sem.at[k, 1])
        total = plain([w_b[k, t] for t in range(G1)])
        w_c_s[k] = total
        w_c[k, m] = total

        def send(j, _):
            t = (m + j) % G2
            remote(
                w_c_s.at[k], w_c.at[k, m], w_send_sem.at[k, 2], w_recv_sem.at[k, 2],
                (2 * t + row % 2, col),
            ).start()
            return 0

        lax.fori_loop(1, G2, send, 0)

    def grad_taps_end(k):
        wait_bytes(w_c.at[k, pl.ds(0, G2 - 1)], w_recv_sem.at[k, 2])
        for t in range(16):
            r, c = 8 * (t // 2), 384 * (t % 2)
            part = w_c[k, t // share, t % share]
            for tap in range(9):
                at = CH * tap - c
                if 0 <= at < 384:
                    gw_ref[k, tap // 3, tap % 3, r : r + 8, :] = part[:, at : at + CH]

    d_one, d_two = dil_ref[0], dil_ref[1]
    moved(0, pin)
    to_channels(pin, S)
    pairs_start()
    move_tile(1, cot_ref, cin, worker)
    pairs_wait()
    spread(
        PAIRS, d_one, lambda e: ext[e].astype(F32), lambda side, g: lat_r[side, g].astype(F32)
    )


    def keep(f):
        def use(i, out, total):
            wide[f, EDGE + i] = out
            return total + out * valid_row(i)

        return use

    nothing = jnp.zeros((CH, CT), F32)
    total = convolve(PAIRS, d_one, 0, keep(FIRST), nothing)
    rows_start(FIRST)

    def beside_first():
        columns_start(FIRST)
        cross_on(0, G2 // 2)

    mean_one, inv_one = norm(0, FIRST, total, beside_first, lambda: corners_start(FIRST))
    scale_one = inv_one * gain_b[0]
    shift_one = shift_b[0]

    def activate(raw, valid):
        level = (raw - mean_one) * scale_one + shift_one
        low = jnp.exp(jnp.minimum(level, 0.0))
        return jnp.where(level > 0.0, level, low - 1.0) * valid, low * valid

    def active_row(e):
        active, slope = activate(wide[FIRST, e], valid_wide(e))
        slope_one[e] = slope
        return active

    def active_beside(side, g):
        return activate(beside_r[FIRST, side, g], valid_beside(side, g))[0]

    field_wait(FIRST)
    spread(ACTIVE, d_two, active_row, active_beside)
    cross_on(G2 // 2, G2)
    total = convolve(ACTIVE, d_two, 2, keep(SECOND), nothing)
    rows_start(SECOND)

    def join_cotangent():
        corners_start(SECOND)
        moved(1, cin)
        mirror_wait(0)

        def join(g, _):
            def use(c, flip):
                back = (cin[c].astype(F32) + flip) * 0.5
                Sb[pl.ds(pl.multiple_of(RT * c, RT), RT), :] = back

            mirror_step(0, g, use)
            return 0

        lax.fori_loop(0, 16, join, 0)

    mean_two, inv_two = norm(2, SECOND, total, lambda: columns_start(SECOND), join_cotangent)
    gain_two = gain_b[1]
    scale_two = inv_two * gain_two
    shift_two = shift_b[1]

    def finish(i, carry):
        p_sum, q_sum = carry
        off = wide[SECOND, EDGE + i] - mean_two
        before = own_row(PAIRS, i).astype(F32) + (off * scale_two + shift_two)
        low = jnp.exp(jnp.minimum(before, 0.0))
        valid = valid_row(i)
        S[pl.ds(i, CH, stride=RT), :] = jnp.where(before > 0.0, before, low - 1.0) * valid
        out = Sb[pl.ds(i, CH, stride=RT), :] * valid * low
        wide[OUTER, EDGE + i] = out
        scaled = out * gain_two
        return p_sum + scaled, q_sum + scaled * (off * inv_two)

    p_sum, q_sum = lax.fori_loop(0, RT, finish, (nothing, nothing), unroll=4)
    rows_start(OUTER)

    def send_final():
        columns_start(OUTER)

        def keep_final(g, _):
            block = S[pl.ds(pl.multiple_of(128 * g, 128), 128), :]
            fin_out[pl.ds(4 * g, 4)] = block.reshape(4, RT, CT).astype(BF16)
            return 0

        lax.fori_loop(0, 16, keep_final, 0)
        move_tile(2, fin_out.at[lower_half], fin_in.at[lower_half], keeper)
        move_tile(3, fin_out.at[upper_half], fin_in.at[upper_half], keeper)
        mirror_pack(1, S)

    def after_final():
        corners_start(OUTER)
        mirror_half(0, 0)
        mirror_half(0, 1)
        mirror_half(1, 0)
        mirror_half(1, 1)
        field_wait(SECOND)

    totals = sums(4, to_message(p_sum, q_sum), send_final, after_final)
    p_two, q_two = from_message(totals / count)

    def grad_two(second, outer, valid):
        normed = (second - mean_two) * inv_two
        return valid * inv_two * (outer * gain_two - p_two - normed * q_two)

    field_wait(OUTER)
    spread(
        GRAD_TWO,
        d_two,
        lambda e: grad_two(wide[SECOND, e], wide[OUTER, e], valid_wide(e)),
        lambda side, g: grad_two(
            beside_r[SECOND, side, g], beside_r[OUTER, side, g], valid_beside(side, g)
        ),
    )
    gain_one = gain_b[0]

    def descend(i, out, carry):
        p_sum, q_sum = carry
        up_i = out * slope_one[EDGE + i]
        wide[INNER, EDGE + i] = up_i
        scaled = up_i * gain_one
        return p_sum + scaled, q_sum + scaled * ((wide[FIRST, EDGE + i] - mean_one) * inv_one)

    p_sum, q_sum = convolve(GRAD_TWO, d_two, 3, descend, (nothing, nothing))
    rows_start(INNER)

    def after_inner():
        corners_start(INNER)
        grad_taps_across(1)

    def beside_inner():
        columns_start(INNER)
        grad_taps(1, ACTIVE, d_two, GRAD_TWO)

    totals = sums(6, to_message(p_sum, q_sum), beside_inner, after_inner)
    p_one, q_one = from_message(totals / count)

    def grad_one(first, inner, valid):
        normed = (first - mean_one) * inv_one
        return valid * inv_one * (inner * gain_one - p_one - normed * q_one)

    field_wait(INNER)
    mirror_half(2, 0)
    mirror_half(2, 1)
    mirror_half(3, 0)
    mirror_half(3, 1)
    spread(
        GRAD_ONE,
        d_one,
        lambda e: grad_one(wide[FIRST, e], wide[INNER, e], valid_wide(e)),
        lambda side, g: grad_one(
            beside_r[FIRST, side, g], beside_r[INNER, side, g], valid_beside(side, g)
        ),
    )
    grad_taps(0, PAIRS, d_one, GRAD_ONE)
    grad_taps_back(1)

    def lower(i, out, carry):
        S[pl.ds(i, CH, stride=RT), :] = (wide[OUTER, EDGE + i] + out) * valid_row(i)
        return carry

    convolve(GRAD_ONE, d_one, 1, lower, 0)

    def keep_grad(g, _):
        block = S[pl.ds(pl.multiple_of(128 * g, 128), 128), :]
        gp_out[pl.ds(4 * g, 4)] = block.reshape(4, RT, CT).astype(BF16)
        return 0

    lax.fori_loop(0, 16, keep_grad, 0)
    grad_taps_across(0)
    move_tile(4, gp_out.at[lower_half], gp_ref.at[lower_half], keeper)
    move_tile(5, gp_out.at[upper_half], gp_ref.at[upper_half], keeper)
    moved(2, fin_in.at[lower_half])
    moved(3, fin_in.at[upper_half])
    mirror_wait(1)

    def join_final(g, _):
        def use(c, flip):
            sym_ref[c] = ((fin_in[c].astype(F32) + flip) * 0.5).astype(BF16)

        mirror_step(1, g, use)
        return 0

    lax.fori_loop(0, 16, join_final, 0)
    grad_taps_back(0)
    grad_taps_end(1)
    grad_taps_end(0)

    sent_tile(0, pin, worker)
    sent_tile(1, cin, worker)
    for k in (2, 3, 4, 5):
        sent_tile(k, fin_out.at[lower_half], keeper)
    cross_sent()
    mirror_sent()
    for q in range(8):
        size = G2 if q % 2 else G1
        wait_bytes(ar_r.at[q, pl.ds(0, size - 1)], ar_send_sem.at[q])
    for k in range(2):
        wait_bytes(w_a.at[k, pl.ds(0, G2 - 1)], w_send_sem.at[k, 0])
        wait_bytes(w_b.at[k, pl.ds(0, G1 - 1)], w_send_sem.at[k, 1])
        wait_bytes(w_c.at[k, pl.ds(0, G2 - 1)], w_send_sem.at[k, 2])
    moved(4, gp_out.at[lower_half])
    moved(5, gp_out.at[upper_half])


def solution(mesh):
    R, C = mesh.shape["row"], mesh.shape["col"]

    def per_device(pairs, w_first, w_second, gains, shifts, dilations, residue_count, cotangent):
        CH, RT, CT = pairs.shape
        G1, G2 = 2 * C, R // 2
        G, share = max(G1, G2), 16 // G2
        vmem = pl.BlockSpec(memory_space=pltpu.VMEM)
        smem = pl.BlockSpec(memory_space=pltpu.SMEM)
        anywhere = pl.BlockSpec(memory_space=pl.ANY)
        tile = pltpu.VMEM((CH, RT, CT), BF16)
        flat = pltpu.VMEM((CH * RT, CT), F32)
        dma = pltpu.SemaphoreType.DMA
        return pl.pallas_call(
            functools.partial(kernel, R, C),
            out_shape=(
                jax.ShapeDtypeStruct((CH, RT, CT), BF16),
                jax.ShapeDtypeStruct((CH, RT, CT), BF16),
                jax.ShapeDtypeStruct((2, 3, 3, CH, CH), F32),
            ),
            in_specs=[smem, smem, anywhere, vmem, vmem, vmem, vmem, vmem],
            out_specs=(vmem, anywhere, vmem),
            scratch_shapes=[
                tile,
                tile,
                tile,
                tile,
                tile,
                pltpu.VMEM((2, 4, 16, RT, CT), BF16),
                pltpu.VMEM((2, 4, 16, RT, CT), BF16),
                pltpu.VMEM((G2, 16, RT, CT), BF16),
                pltpu.VMEM((RT + 2 * EDGE, CH, CT), BF16),
                pltpu.VMEM((2, 4, CH, CT), BF16),
                pltpu.VMEM((2, 8, CH, CT), BF16),
                pltpu.VMEM((4, RT + 2 * EDGE, 3 * CH, CT), BF16),
                flat,
                flat,
                pltpu.VMEM((4, RT + 2 * EDGE, CH, CT), F32),
                pltpu.VMEM((4, 2, 4, CH, CT), F32),
                pltpu.VMEM((4, 2, 8, CH, CT), F32),
                pltpu.VMEM((RT + 2 * EDGE, CH, CT), F32),
                pltpu.VMEM((4, CH, 9 * CH), BF16),
                pltpu.VMEM((2, CH, CT), F32),
                pltpu.VMEM((2, CH, CT), F32),
                pltpu.VMEM((8, 1, CT), F32),
                pltpu.VMEM((8, G, 1, CT), F32),
                pltpu.VMEM((CH, 768), F32),
                pltpu.VMEM((2, G2, share, 8, 384), F32),
                pltpu.VMEM((2, G2, share, 8, 384), F32),
                pltpu.VMEM((2, share, 8, 384), F32),
                pltpu.VMEM((2, G1, share, 8, 384), F32),
                pltpu.VMEM((2, share, 8, 384), F32),
                pltpu.VMEM((2, G2, share, 8, 384), F32),
                dma((6,)),
                dma((6,)),
                dma((5, 8)),
                dma((5, 8)),
                dma((2, 8)),
                dma((2, 8)),
                dma((8,)),
                dma((8,)),
                dma((G2,)),
                dma((G2,)),
                dma((2, 3)),
                dma((2, 3)),
            ],
            compiler_params=pltpu.CompilerParams(
                collective_id=0, has_side_effects=True, vmem_limit_bytes=56 * 1024 * 1024
            ),
            cost_estimate=pl.CostEstimate(
                flops=6 * 2 * 9 * CH * CH * RT * CT, bytes_accessed=4 * CH * RT * CT, transcendentals=0
            ),
        )(dilations, residue_count, pairs, cotangent, w_first, w_second, gains, shifts)

    in_specs = (P(None, "row", "col"), P(), P(), P(), P(), P(), P(), P(None, "row", "col"))
    out_specs = (P(None, "row", "col"), P(None, "row", "col"), P())
    return jax.shard_map(
        per_device, mesh=mesh, in_specs=in_specs, out_specs=out_specs, check_vma=False
    )
```
